32 devices in a mesh: row: 8 (over y, x, core), col: 4 (over z).
Axes of the slice: x: 2, y: 2, z: 4, core: 2. Of those that a mesh axis runs over, the one named last changes fastest.
Arguments:
- picture_encoder_output: bfloat16 [6144, 1152], P(('row', 'col')), may hold values from -0.59765625 to 0.59765625
- caption_encoder_output: bfloat16 [6144, 1152], P(('row', 'col')), may hold values from -0.59765625 to 0.59765625
- softness_factor_exponent: float32 [], replicated, may hold values from 2.7 to 3.7
- logit_offset_term: float32 [], replicated, may hold values from -5 to -2
Outputs:
- image_grad: float32 [6144, 1152], P(('row', 'col'))
- text_grad: float32 [6144, 1152], P(('row', 'col'))
The draws below stay inside these ranges and needn't reach their ends.
All inputs are finite; a program needn't handle non-finite values.
Results may differ from the reference program's by a relative error of at most 0.008.
Values may be sent and summed in bfloat16 or wider, within the bound.
No kernel may reach another device: no remote copies, remote signals or barrier semaphores. Data moves between devices by JAX's collectives and lax.ppermute only.
A program may use at most 64 MiB of HBM per device.

```python
import jax
import jax.numpy as jnp
from jax import lax

EMBED = 1152
ROWS_DEV = 192
SPAN_ROW = 4
SPAN_COL = 2
BATCH = 6144
N_ROW = 8
N_COL = 4


def block_levels(rng, dims, cuts, least, high):
    level = 1.0
    for dim, shards_of in cuts:
        steps = jax.random.uniform(jax.random.fold_in(jax.random.fold_in(rng, 6), dim), (shards_of,), jnp.float32, least / len(cuts), high / len(cuts))
        level = level * jnp.repeat(jnp.exp(steps), dims[dim] // shards_of).reshape((-1,) + (1,) * (len(dims) - 1 - dim))
    return level


def noise(rng, shape, spread, reach, split=(), held_as=jnp.bfloat16):
    drawn = spread * jax.random.normal(rng, shape, jnp.float32)
    if split:
        drawn = drawn * block_levels(rng, shape, split, -0.22, 0.18)
    return jnp.clip(drawn, -reach, reach).astype(held_as)


def setup_inputs(seed: int = 0) -> dict:
    seeds = jax.random.split(jax.random.key(seed), 5)
    return {
        "picture_encoder_output": noise(seeds[0], (BATCH, EMBED), 0.1, 0.59765625, ((0, 32),)),
        "caption_encoder_output": noise(seeds[1], (BATCH, EMBED), 0.1, 0.59765625, ((0, 32),)),
        "softness_factor_exponent": jnp.clip(jax.random.uniform(seeds[2], (), jnp.float32, 2.7, 3.7), 2.7, 3.7),
        "logit_offset_term": jnp.clip(jax.random.uniform(seeds[3], (), jnp.float32, -5.0, -2.0), -5.0, -2.0),
    }


eps_norm = 1e-06

def unit_rows(feature):
    values = feature.astype(jnp.float32)
    inverse = lax.rsqrt(lax.optimization_barrier(jnp.sum(values * values, axis=-1, keepdims=True)) + eps_norm)
    return (values * inverse, inverse)

def unit_back(unit, inverse, direction):
    along = lax.optimization_barrier(jnp.sum(unit * direction, axis=-1, keepdims=True))
    return inverse * (direction - unit * along)

def reference(picture_encoder_output, caption_encoder_output, softness_factor_exponent, logit_offset_term):
    img_unit, img_inv = unit_rows(picture_encoder_output)
    txt_unit, text_inverse_norm = unit_rows(caption_encoder_output)
    img_half = img_unit.astype(jnp.bfloat16)
    txt_half = txt_unit.astype(jnp.bfloat16)
    trained_softness_factor = jnp.exp(softness_factor_exponent.astype(jnp.float32))
    images = img_half.astype(jnp.float32).reshape(N_ROW, N_COL, ROWS_DEV, EMBED)
    texts = txt_half.astype(jnp.float32).reshape(N_ROW, N_COL, ROWS_DEV, EMBED)
    diagonal = jnp.eye(ROWS_DEV, dtype=jnp.float32)

    def meet(img_block, match_target_sign):
        matched_cosine_scores = jnp.einsum('abie,abje->abij', img_block, texts)
        matched_loss_multipliers = (trained_softness_factor * (jax.nn.sigmoid(trained_softness_factor * matched_cosine_scores + logit_offset_term) - match_target_sign)).astype(jnp.bfloat16)
        matched_loss_multipliers = matched_loss_multipliers.astype(jnp.float32)
        img_part = jnp.einsum('abij,abje->abie', matched_loss_multipliers, texts)
        txt_part = jnp.einsum('abij,abie->abje', matched_loss_multipliers, img_block)
        return (img_part, txt_part)
    img_dir = jnp.zeros((N_ROW, N_COL, ROWS_DEV, EMBED), jnp.float32)
    txt_dir = jnp.zeros((N_ROW, N_COL, ROWS_DEV, EMBED), jnp.float32)
    for offset in range(SPAN_ROW):
        match_target_sign = diagonal if offset == 0 else 0.0
        img_part, txt_part = meet(jnp.roll(images, -offset, axis=0), match_target_sign)
        img_dir = img_dir + jnp.roll(img_part, offset, axis=0)
        txt_dir = txt_dir + txt_part
    for offset in range(1, SPAN_COL):
        img_part, txt_part = meet(jnp.roll(images, -offset, axis=1), 0.0)
        img_dir = img_dir + jnp.roll(img_part, offset, axis=1)
        txt_dir = txt_dir + txt_part
    img_dir = img_dir.reshape(BATCH, EMBED)
    txt_dir = txt_dir.reshape(BATCH, EMBED)
    return (unit_back(img_unit, img_inv, img_dir), unit_back(txt_unit, text_inverse_norm, txt_dir))
```

```python
import jax
import jax.numpy as jnp
from jax import lax
from jax.sharding import PartitionSpec as P

eps_norm = 1e-06


def along(value, axis, target):
    count = lax.axis_size(axis)
    pairs = [(source, target(source) % count) for source in range(count)]
    return lax.ppermute(value, axis, pairs)


def unit_rows(feature):
    values = feature.astype(jnp.float32)
    inverse = lax.rsqrt(jnp.sum(values * values, axis=-1, keepdims=True) + eps_norm)
    return (values * inverse, inverse)


def unit_half(feature):
    return unit_rows(feature)[0].astype(jnp.bfloat16)


def unit_back(unit, inverse, direction):
    along = jnp.sum(unit * direction, axis=-1, keepdims=True)
    return inverse * (direction - unit * along)


def row_blocks(img, txt, extent):
    texts, images = [], []
    if extent % 2 or lax.axis_size("row") % 2:
        for k in range(1, extent):
            texts.append(along(txt, "row", lambda s: s + k))
            images.append(along(img, "row", lambda s: s - k))
        return texts, images
    odd = lax.axis_index("row") % 2 == 1
    swap = lambda s: s ^ 1
    for d in range(2, extent, 2):
        texts.append(along(txt, "row", lambda s: s + d))
        images.append(along(img, "row", lambda s: s - d))
    reach = extent - 1
    far = along(jnp.where(odd, txt, img), "row", lambda s: s + reach if s % 2 else s - reach)
    near = along(jnp.where(odd, img, txt), "row", swap)
    texts += [along(t, "row", swap) for t in texts]
    images += [along(t, "row", swap) for t in images]
    texts.append(jnp.where(odd, near, far))
    images.append(jnp.where(odd, far, near))
    return texts, images


def on_device(
    picture_encoder_output, caption_encoder_output, softness_factor_exponent, logit_offset_term
):
    img, txt = picture_encoder_output, caption_encoder_output
    row_extent = min(8, lax.axis_size("row") // 2)
    column_extent = min(4, lax.axis_size("col") // 2)
    texts, images = [], []
    for k in range(1, column_extent):
        texts.append(along(txt, "col", lambda s: s + k))
        images.append(along(img, "col", lambda s: s - k))
    more_texts, more_images = row_blocks(img, txt, row_extent)
    texts += more_texts
    images += more_images
    temperature = jnp.exp(softness_factor_exponent)
    diagonal = jnp.eye(img.shape[0], dtype=jnp.float32)

    def visit(own, other, match):
        scores = lax.dot_general(
            own, other, (((1,), (1,)), ((), ())), preferred_element_type=jnp.float32
        )
        weights = temperature * (jax.nn.sigmoid(temperature * scores + logit_offset_term) - match)
        return jnp.dot(weights.astype(jnp.bfloat16), other, preferred_element_type=jnp.float32)

    img_unit, img_inv = unit_rows(img)
    txt_unit, txt_inv = unit_rows(txt)
    img_half = img_unit.astype(jnp.bfloat16)
    txt_half = txt_unit.astype(jnp.bfloat16)
    img_dir = visit(img_half, txt_half, diagonal)
    txt_dir = visit(txt_half, img_half, diagonal)
    for block in texts:
        img_dir = img_dir + visit(img_half, unit_half(block), 0.0)
    for block in images:
        txt_dir = txt_dir + visit(txt_half, unit_half(block), 0.0)
    return (unit_back(img_unit, img_inv, img_dir), unit_back(txt_unit, txt_inv, txt_dir))


def solution(mesh):
    return jax.shard_map(
        on_device,
        mesh=mesh,
        in_specs=(P(("row", "col"), None), P(("row", "col"), None), P(), P()),
        out_specs=(P(("row", "col"), None), P(("row", "col"), None)),
        check_vma=False,
    )
```

```python
import functools

import jax
import jax.numpy as jnp
from jax import lax
from jax.experimental import pallas as pl
from jax.experimental.pallas import tpu as pltpu
from jax.sharding import PartitionSpec as P

eps_norm = 1e-06
VMEM = pl.BlockSpec(memory_space=pltpu.VMEM)
SMEM = pl.BlockSpec(memory_space=pltpu.SMEM)
ANY = pl.BlockSpec(memory_space=pl.ANY)
LIMIT = 24 * 2**20


def along(value, axis, target):
    count = lax.axis_size(axis)
    pairs = [(source, target(source) % count) for source in range(count)]
    return lax.ppermute(value, axis, pairs)


def inverse_norm(values):
    return lax.rsqrt(jnp.sum(values * values, axis=-1, keepdims=True) + eps_norm)


def unit_half(raw):
    values = raw.astype(jnp.float32)
    return (values * inverse_norm(values)).astype(jnp.bfloat16)


def weigh(own, other, temperature, offset):
    scores = lax.dot_general(
        own, other, (((1,), (1,)), ((), ())), preferred_element_type=jnp.float32
    )
    return jax.nn.sigmoid(temperature * scores + offset)


def visit(own, raw, temperature, offset):
    other = unit_half(raw)
    weights = temperature * weigh(own, other, temperature, offset)
    return jnp.dot(weights.astype(jnp.bfloat16), other, preferred_element_type=jnp.float32)


def unit_back(raw, direction):
    values = raw.astype(jnp.float32)
    inverse = inverse_norm(values)
    unit = values * inverse
    share = jnp.sum(unit * direction, axis=-1, keepdims=True)
    return inverse * (direction - unit * share)


def cost(rows, width, products, arrays):
    return pl.CostEstimate(
        flops=2 * rows * rows * width * products,
        bytes_accessed=2 * rows * width * arrays,
        transcendentals=0,
    )


def place(side, odd_ref):
    return side if side < 2 else odd_ref[0] if side == 2 else 1 - odd_ref[0]


def copy_all(pairs, sems):
    copies = [pltpu.make_async_copy(a, b, sems.at[n]) for n, (a, b) in enumerate(pairs)]
    for copy in copies:
        copy.start()
    for copy in copies:
        copy.wait()


def far_kernel(odd_ref, img_ref, txt_ref, out_ref, sems):
    @pl.when(odd_ref[0] == 1)
    def _():
        copy_all([(txt_ref, out_ref)], sems)

    @pl.when(odd_ref[0] != 1)
    def _():
        copy_all([(img_ref, out_ref)], sems)


def near_kernel(odd_ref, img_ref, txt_ref, block_ref, out_ref, sems):
    @pl.when(odd_ref[0] == 1)
    def _():
        copy_all([(block_ref, out_ref.at[0]), (img_ref, out_ref.at[1])], sems)

    @pl.when(odd_ref[0] != 1)
    def _():
        copy_all([(block_ref, out_ref.at[0]), (txt_ref, out_ref.at[1])], sems)


def pick(kernel, odd, *blocks):
    shape = blocks[0].shape if len(blocks) == 2 else (2,) + blocks[0].shape
    return pl.pallas_call(
        kernel,
        out_shape=jax.ShapeDtypeStruct(shape, blocks[0].dtype),
        in_specs=[SMEM] + [ANY] * len(blocks),
        out_specs=ANY,
        scratch_shapes=[pltpu.SemaphoreType.DMA((2,))],
        compiler_params=pltpu.CompilerParams(vmem_limit_bytes=48 * 2**20),
        cost_estimate=cost(*blocks[0].shape, 0, 2 * len(blocks) - 2),
        name="pick",
    )(odd, *blocks)


def own_kernel(scale_ref, img_ref, txt_ref, half_ref, dir_ref):
    temperature, offset = scale_ref[0], scale_ref[1]
    half_ref[0] = unit_half(img_ref[...])
    half_ref[1] = unit_half(txt_ref[...])
    img, txt = half_ref[0], half_ref[1]
    rows = img.shape[0]
    row = lax.broadcasted_iota(jnp.int32, (rows, rows), 0)
    column = lax.broadcasted_iota(jnp.int32, (rows, rows), 1)
    match = jnp.where(row == column, 1.0, 0.0)
    weights = (temperature * (weigh(img, txt, temperature, offset) - match)).astype(jnp.bfloat16)
    dir_ref[0] = jnp.dot(weights, txt, preferred_element_type=jnp.float32)
    weights = (temperature * (weigh(txt, img, temperature, offset) - match)).astype(jnp.bfloat16)
    dir_ref[1] = jnp.dot(weights, img, preferred_element_type=jnp.float32)


def own_visit(scale, img, txt):
    rows, width = img.shape
    return pl.pallas_call(
        own_kernel,
        out_shape=(
            jax.ShapeDtypeStruct((2, rows, width), jnp.bfloat16),
            jax.ShapeDtypeStruct((2, rows, width), jnp.float32),
        ),
        in_specs=[SMEM, VMEM, VMEM],
        out_specs=(VMEM, VMEM),
        compiler_params=pltpu.CompilerParams(vmem_limit_bytes=LIMIT),
        cost_estimate=cost(rows, width, 4, 8),
        name="own",
    )(scale, img, txt)


def visit_all(sides, blocks, scale_ref, odd_ref, half_ref, out_ref):
    for held, block in zip(sides, blocks):
        for n, side in enumerate(held):
            raw = block[n] if len(held) > 1 else block[...]
            at = place(side, odd_ref)
            out_ref[at] += visit(half_ref[at], raw, scale_ref[0], scale_ref[1])


def more_kernel(sides, scale_ref, odd_ref, half_ref, dir_ref, *rest):
    blocks, out_ref = rest[:-1], rest[-1]
    out_ref[...] = dir_ref[...]
    visit_all(sides, blocks, scale_ref, odd_ref, half_ref, out_ref)


def more_visits(scale, odd, half, direction, sides, blocks):
    rows, width = half.shape[1:]
    return pl.pallas_call(
        functools.partial(more_kernel, sides),
        out_shape=jax.ShapeDtypeStruct(direction.shape, direction.dtype),
        in_specs=[SMEM, SMEM, VMEM, VMEM] + [VMEM] * len(blocks),
        out_specs=VMEM,
        input_output_aliases={3: 0},
        compiler_params=pltpu.CompilerParams(vmem_limit_bytes=LIMIT),
        cost_estimate=cost(rows, width, 2 * len(blocks), 6 + len(blocks)),
        name="more",
    )(scale, odd, half, direction, *blocks)


def last_kernel(sides, scale_ref, odd_ref, img_ref, txt_ref, half_ref, dir_ref, *rest):
    blocks, (img_grad, txt_grad, acc) = rest[:-3], rest[-3:]
    acc[...] = dir_ref[...]
    visit_all(sides, blocks, scale_ref, odd_ref, half_ref, acc)
    img_grad[...] = unit_back(img_ref[...], acc[0])
    txt_grad[...] = unit_back(txt_ref[...], acc[1])


def last_visits(scale, odd, img, txt, half, direction, sides, blocks):
    rows, width = img.shape
    grad = jax.ShapeDtypeStruct((rows, width), jnp.float32)
    return pl.pallas_call(
        functools.partial(last_kernel, sides),
        out_shape=(grad, grad),
        in_specs=[SMEM, SMEM] + [VMEM] * (4 + len(blocks)),
        out_specs=(VMEM, VMEM),
        scratch_shapes=[pltpu.VMEM((2, rows, width), jnp.float32)],
        compiler_params=pltpu.CompilerParams(vmem_limit_bytes=LIMIT),
        cost_estimate=cost(rows, width, 2 * len(blocks), 12 + len(blocks)),
        name="last",
    )(scale, odd, img, txt, half, direction, *blocks)


def on_device(
    picture_encoder_output, caption_encoder_output, softness_factor_exponent, logit_offset_term
):
    img, txt = picture_encoder_output, caption_encoder_output
    row_extent = min(8, lax.axis_size("row") // 2)
    column_extent = min(4, lax.axis_size("col") // 2)
    odd = (lax.axis_index("row") & 1).astype(jnp.int32).reshape(1)
    scale = jnp.stack([jnp.exp(softness_factor_exponent), logit_offset_term])
    paired = row_extent % 2 == 0 and lax.axis_size("row") % 2 == 0
    swap = lambda s: s ^ 1

    half, direction = own_visit(scale, img, txt)

    def add(blocks):
        if not blocks:
            return direction
        return more_visits(scale, odd, half, direction, *zip(*blocks))

    def tied(blocks, *others):
        arrays, others = lax.optimization_barrier(([block for _, block in blocks], others))
        return [(side, block) for (side, _), block in zip(blocks, arrays)], *others

    early, first, late, swapped = [], [], [], []
    for k in range(1, column_extent):
        early.append(((0,), along(txt, "col", lambda s: s + k)))
        late.append(((1,), along(img, "col", lambda s: s - k)))
    if paired:
        for d in range(2, row_extent, 2):
            first.append(((0,), along(txt, "row", lambda s: s + d)))
            late.append(((1,), along(img, "row", lambda s: s - d)))
        reach = row_extent - 1
        far = pick(far_kernel, odd, img, txt)
        late.append(((2,), along(far, "row", lambda s: s + reach if s % 2 else s - reach)))
        direction = add(early)
        first, direction = tied(first, direction)
        for n, (side, block) in enumerate(first):
            if n == 0:
                block = pick(near_kernel, odd, img, txt, block)
                side += (3,)
            swapped.append((side, along(block, "row", swap)))
        if not first:
            near = pick(far_kernel, 1 - odd, img, txt)
            swapped.append(((3,), along(near, "row", swap)))
        late, = tied(late)
        for side, block in late[column_extent - 1 : -1]:
            swapped.append((side, along(block, "row", swap)))
        direction = add(first + late)
    else:
        swapped = early + late
        for k in range(1, row_extent):
            swapped.append(((0,), along(txt, "row", lambda s: s + k)))
            swapped.append(((1,), along(img, "row", lambda s: s - k)))

    sides, blocks = zip(*swapped) if swapped else ((), ())
    return last_visits(scale, odd, img, txt, half, direction, sides, blocks)


def solution(mesh):
    return jax.shard_map(
        on_device,
        mesh=mesh,
        in_specs=(P(("row", "col"), None), P(("row", "col"), None), P(), P()),
        out_specs=(P(("row", "col"), None), P(("row", "col"), None)),
        check_vma=False,
    )
```

```python
import functools

import jax
import jax.numpy as jnp
from jax import lax
from jax.experimental import pallas as pl
from jax.experimental.pallas import tpu as pltpu
from jax.sharding import PartitionSpec as P

eps_norm = 1e-06
VMEM = pl.BlockSpec(memory_space=pltpu.VMEM)
SMEM = pl.BlockSpec(memory_space=pltpu.SMEM)
HBM = pl.BlockSpec(memory_space=pltpu.HBM)
LIMIT = 24 * 2**20
PIECES = 4


def along(value, axis, target):
    count = lax.axis_size(axis)
    pairs = [(source, target(source) % count) for source in range(count)]
    return lax.ppermute(value, axis, pairs)


def inverse_norm(values):
    return lax.rsqrt(jnp.sum(values * values, axis=-1, keepdims=True) + eps_norm)


def unit_half(raw):
    values = raw.astype(jnp.float32)
    return (values * inverse_norm(values)).astype(jnp.bfloat16)


def weigh(own, other, temperature, offset):
    scores = lax.dot_general(
        own, other, (((1,), (1,)), ((), ())), preferred_element_type=jnp.float32
    )
    return jax.nn.sigmoid(temperature * scores + offset)


def visit(own, other, temperature, offset):
    weights = temperature * weigh(own, other, temperature, offset)
    return jnp.dot(weights.astype(jnp.bfloat16), other, preferred_element_type=jnp.float32)


def unit_back(raw, direction):
    values = raw.astype(jnp.float32)
    inverse = inverse_norm(values)
    unit = values * inverse
    share = jnp.sum(unit * direction, axis=-1, keepdims=True)
    return inverse * (direction - unit * share)


def pieces(rows):
    if rows % (16 * PIECES):
        return [(0, rows)]
    return [(n * rows // PIECES, rows // PIECES) for n in range(PIECES)]


def call(kernel, out_shape, in_specs, out_specs, **more):
    return pl.pallas_call(
        kernel,
        out_shape=out_shape,
        in_specs=in_specs,
        out_specs=out_specs,
        compiler_params=pltpu.CompilerParams(vmem_limit_bytes=LIMIT),
        cost_estimate=pl.CostEstimate(flops=1000, bytes_accessed=1000, transcendentals=0),
        **more,
    )


def norm_kernel(odd_ref, img_ref, txt_ref, raw_ref, half_ref, img_half, far_ref, near_ref, sems):
    parts = pieces(img_ref.shape[0])
    copies = []
    for side, source in ((0, img_ref), (1, txt_ref)):
        for n, (start, size) in enumerate(parts):
            at = pl.ds(start, size)
            copies.append(
                pltpu.make_async_copy(source.at[at], raw_ref.at[side, at], sems.at[side, n])
            )
    for copy in copies:
        copy.start()
    for side in (0, 1):
        for n, (start, size) in enumerate(parts):
            copies[side * len(parts) + n].wait()
            at = pl.ds(start, size)
            half_ref[side, at] = unit_half(raw_ref[side, at])
            if side == 0:
                img_half[at] = half_ref[side, at]
    far_ref[...] = half_ref[odd_ref[0]]
    near_ref[...] = half_ref[1 - odd_ref[0]]


def norm(odd, img, txt):
    rows, width = img.shape
    one = jax.ShapeDtypeStruct((rows, width), jnp.bfloat16)
    both = jax.ShapeDtypeStruct((2, rows, width), jnp.bfloat16)
    return call(
        norm_kernel,
        (both, both, one, one, one),
        [SMEM, HBM, HBM],
        (VMEM,) * 5,
        scratch_shapes=[pltpu.SemaphoreType.DMA((2, len(pieces(rows))))],
        name="norm",
    )(odd, img, txt)


def own_kernel(scale_ref, half_ref, dir_ref):
    temperature, offset = scale_ref[0], scale_ref[1]
    img, txt = half_ref[0], half_ref[1]
    rows = img.shape[0]
    row = lax.broadcasted_iota(jnp.int32, (rows, rows), 0)
    column = lax.broadcasted_iota(jnp.int32, (rows, rows), 1)
    match = jnp.where(row == column, 1.0, 0.0)
    weights = (temperature * (weigh(img, txt, temperature, offset) - match)).astype(jnp.bfloat16)
    dir_ref[0] = jnp.dot(weights, txt, preferred_element_type=jnp.float32)
    weights = (temperature * (weigh(txt, img, temperature, offset) - match)).astype(jnp.bfloat16)
    dir_ref[1] = jnp.dot(weights, img, preferred_element_type=jnp.float32)


def own_visit(scale, half):
    return call(
        own_kernel,
        jax.ShapeDtypeStruct(half.shape, jnp.float32),
        [SMEM, VMEM],
        VMEM,
        name="own",
    )(scale, half)


def visit_all(kinds, blocks, scale_ref, odd_ref, half_ref, acc_ref):
    for (side, raw), block in zip(kinds, blocks):
        other = unit_half(block[...]) if raw else block[...]
        at = side if side < 2 else odd_ref[0] if side == 2 else 1 - odd_ref[0]
        acc_ref[at] += visit(half_ref[at], other, scale_ref[0], scale_ref[1])


def more_kernel(kinds, scale_ref, odd_ref, half_ref, dir_ref, *rest):
    blocks, out_ref = rest[:-1], rest[-1]
    out_ref[...] = dir_ref[...]
    visit_all(kinds, blocks, scale_ref, odd_ref, half_ref, out_ref)


def finish(raw_ref, acc_ref, grad_ref, held_ref, sems):
    copies = []
    for n, (start, size) in enumerate(pieces(held_ref.shape[0])):
        at = pl.ds(start, size)
        held_ref[at] = unit_back(raw_ref[at], acc_ref[at])
        copies.append(pltpu.make_async_copy(held_ref.at[at], grad_ref.at[at], sems.at[n]))
        copies[-1].start()
    return copies


def image_kernel(kinds, scale_ref, odd_ref, half_ref, dir_ref, raw_ref, *rest):
    blocks, (out_ref, grad_ref, held_ref, sems) = rest[:-4], rest[-4:]
    out_ref[...] = dir_ref[...]
    visit_all(kinds, blocks, scale_ref, odd_ref, half_ref, out_ref)
    for copy in finish(raw_ref.at[0], out_ref.at[0], grad_ref, held_ref, sems):
        copy.wait()


def text_kernel(kinds, scale_ref, odd_ref, half_ref, dir_ref, raw_ref, *rest):
    blocks, (grad_ref, acc_ref, held_ref, sems) = rest[:-4], rest[-4:]
    acc_ref[1] = dir_ref[1]
    visit_all(kinds, blocks, scale_ref, odd_ref, half_ref, acc_ref)
    for copy in finish(raw_ref.at[1], acc_ref.at[1], grad_ref, held_ref, sems):
        copy.wait()


def visits(kernel, scale, odd, half, direction, entries, raw=None):
    kinds, blocks = zip(*entries) if entries else ((), ())
    rows, width = half.shape[1:]
    same = jax.ShapeDtypeStruct(direction.shape, direction.dtype)
    grad = jax.ShapeDtypeStruct((rows, width), jnp.float32)
    operands = [scale, odd, half, direction] + ([] if raw is None else [raw])
    held = [pltpu.VMEM(grad.shape, grad.dtype), pltpu.SemaphoreType.DMA((len(pieces(rows)),))]
    if kernel is more_kernel:
        out_shape, out_specs, held, aliases = same, VMEM, [], {3: 0}
    elif kernel is image_kernel:
        out_shape, out_specs, aliases = (same, grad), (VMEM, HBM), {3: 0}
    else:
        out_shape, out_specs, aliases = grad, HBM, {}
        held = [pltpu.VMEM(same.shape, same.dtype)] + held
    return call(
        functools.partial(kernel, kinds),
        out_shape,
        [SMEM, SMEM] + [VMEM] * (len(operands) - 2 + len(blocks)),
        out_specs,
        input_output_aliases=aliases,
        scratch_shapes=held,
        name=kernel.__name__,
    )(*operands, *blocks)


def on_device(
    picture_encoder_output, caption_encoder_output, softness_factor_exponent, logit_offset_term
):
    img, txt = picture_encoder_output, caption_encoder_output
    row_extent = min(8, lax.axis_size("row") // 2)
    column_extent = min(4, lax.axis_size("col") // 2)
    odd = (lax.axis_index("row") & 1).astype(jnp.int32).reshape(1)
    scale = jnp.stack([jnp.exp(softness_factor_exponent), logit_offset_term])
    paired = row_extent % 2 == 0 and lax.axis_size("row") % 2 == 0
    swap = lambda s: s ^ 1
    held = [pltpu.with_memory_space_constraint(a, pltpu.HBM) for a in (img, txt)]
    raw, half, img_half, far, near = norm(odd, *held)

    def tied(entries, *others):
        blocks, others = lax.optimization_barrier(([block for _, block in entries], others))
        return [(kind, block) for (kind, _), block in zip(entries, blocks)], *others

    text_cols, image_cols, text_rows, image_rows, swapped, last = [], [], [], [], [], []
    for k in range(1, column_extent):
        text_cols.append(((0, True), along(txt, "col", lambda s: s + k)))
    direction = own_visit(scale, half)
    tied_cols, col_half, direction = tied(text_cols, img_half, direction)
    for k in range(1, column_extent):
        image_cols.append(((1, False), along(col_half, "col", lambda s: s - k)))
    direction = visits(more_kernel, scale, odd, half, direction, tied_cols)
    if paired:
        for d in range(2, row_extent, 2):
            text_rows.append(((0, True), along(txt, "row", lambda s: s + d)))
            image_rows.append(((1, False), along(img_half, "row", lambda s: s - d)))
        reach = row_extent - 1
        far = [((2, False), along(far, "row", lambda s: s + reach if s % 2 else s - reach))]
        direction = visits(more_kernel, scale, odd, half, direction, text_rows)
        tied_rows, near, direction = tied(text_rows, near, direction)
        swapped.append(((3, False), along(near, "row", swap)))
        for kind, block in tied_rows:
            swapped.append((kind, along(block, "row", swap)))
        count = len(image_rows)
        rest, direction = tied(image_rows + image_cols + far, direction)
        for kind, block in rest[:count]:
            last.append((kind, along(block, "row", swap)))
        middle = rest + swapped
    else:
        middle = image_cols
        for k in range(1, row_extent):
            middle.append(((0, True), along(txt, "row", lambda s: s + k)))
            middle.append(((1, True), along(img, "row", lambda s: s - k)))

    direction, image_grad = visits(image_kernel, scale, odd, half, direction, middle, raw)
    return image_grad, visits(text_kernel, scale, odd, half, direction, last, raw)


def solution(mesh):
    return jax.shard_map(
        on_device,
        mesh=mesh,
        in_specs=(P(("row", "col"), None), P(("row", "col"), None), P(), P()),
        out_specs=(P(("row", "col"), None), P(("row", "col"), None)),
        check_vma=False,
    )
```

```python
import functools

import jax
import jax.numpy as jnp
from jax import lax
from jax.experimental import pallas as pl
from jax.experimental.pallas import tpu as pltpu
from jax.sharding import PartitionSpec as P

eps_norm = 1e-06
VMEM = pl.BlockSpec(memory_space=pltpu.VMEM)
SMEM = pl.BlockSpec(memory_space=pltpu.SMEM)
HBM = pl.BlockSpec(memory_space=pltpu.HBM)
LIMIT = 24 * 2**20
PIECES = 4


def along(value, axis, target):
    count = lax.axis_size(axis)
    pairs = [(source, target(source) % count) for source in range(count)]
    return lax.ppermute(value, axis, pairs)


def inverse_norm(values):
    return lax.rsqrt(jnp.sum(values * values, axis=-1, keepdims=True) + eps_norm)


def unit_half(raw):
    values = raw.astype(jnp.float32)
    return (values * inverse_norm(values)).astype(jnp.bfloat16)


def weigh(own, other, scale_ref):
    scores = lax.dot_general(
        own, other, (((1,), (1,)), ((), ())), preferred_element_type=jnp.float32
    )
    return jax.nn.sigmoid(scale_ref[0:1, 0:1] * scores + scale_ref[1:2, 0:1])


def visit(own, other, scale_ref):
    weights = scale_ref[0:1, 0:1] * weigh(own, other, scale_ref)
    return jnp.dot(weights.astype(jnp.bfloat16), other, preferred_element_type=jnp.float32)


def odd_row():
    return lax.axis_index("row") & 1


def unit_back(raw, direction):
    values = raw.astype(jnp.float32)
    inverse = inverse_norm(values)
    unit = values * inverse
    share = jnp.sum(unit * direction, axis=-1, keepdims=True)
    return inverse * (direction - unit * share)


def pieces(rows):
    if rows % (16 * PIECES):
        return [(0, rows)]
    return [(n * rows // PIECES, rows // PIECES) for n in range(PIECES)]


def call(kernel, out_shape, in_specs, out_specs, **more):
    return pl.pallas_call(
        kernel,
        out_shape=out_shape,
        in_specs=in_specs,
        out_specs=out_specs,
        compiler_params=pltpu.CompilerParams(vmem_limit_bytes=LIMIT),
        cost_estimate=pl.CostEstimate(flops=1000, bytes_accessed=1000, transcendentals=0),
        **more,
    )


def pick_kernel(img_ref, txt_ref, out_ref, sems):
    def copy(source):
        parts = [pl.ds(start, size) for start, size in pieces(out_ref.shape[0])]
        copies = [
            pltpu.make_async_copy(source.at[at], out_ref.at[at], sems.at[n])
            for n, at in enumerate(parts)
        ]
        for one in copies:
            one.start()
        for one in copies:
            one.wait()

    odd = odd_row()

    @pl.when(odd == 1)
    def _():
        copy(txt_ref)

    @pl.when(odd != 1)
    def _():
        copy(img_ref)


def pick(img, txt):
    return call(
        pick_kernel,
        jax.ShapeDtypeStruct(img.shape, img.dtype),
        [HBM, HBM],
        VMEM,
        scratch_shapes=[pltpu.SemaphoreType.DMA((len(pieces(img.shape[0])),))],
        name="pick",
    )(img, txt)


def norm_kernel(exponent_ref, offset_ref, img_ref, txt_ref, scale_ref, raw_ref, half_ref, near_ref, sems):
    parts = pieces(img_ref.shape[0])
    copies = []
    for side, source in ((0, img_ref), (1, txt_ref)):
        for n, (start, size) in enumerate(parts):
            at = pl.ds(start, size)
            copies.append(
                pltpu.make_async_copy(source.at[at], raw_ref.at[side, at], sems.at[side, n])
            )
    for copy in copies:
        copy.start()
    scale_ref[0:1] = jnp.exp(jnp.full((1, 128), exponent_ref[0], jnp.float32))
    scale_ref[1:2] = jnp.full((1, 128), offset_ref[0], jnp.float32)
    for side in (0, 1):
        for n, (start, size) in enumerate(parts):
            copies[side * len(parts) + n].wait()
            at = pl.ds(start, size)
            half_ref[side, at] = unit_half(raw_ref[side, at])
    near_ref[...] = half_ref[1 - odd_row()]


def norm(exponent, offset, img, txt):
    rows, width = img.shape
    both = jax.ShapeDtypeStruct((2, rows, width), jnp.bfloat16)
    return call(
        norm_kernel,
        (
            jax.ShapeDtypeStruct((8, 128), jnp.float32),
            both,
            both,
            jax.ShapeDtypeStruct((rows, width), jnp.bfloat16),
        ),
        [SMEM, SMEM, HBM, HBM],
        (VMEM,) * 4,
        scratch_shapes=[pltpu.SemaphoreType.DMA((2, len(pieces(rows))))],
        name="norm",
    )(exponent, offset, img, txt)


def own_kernel(scale_ref, half_ref, dir_ref):
    img, txt = half_ref[0], half_ref[1]
    rows = img.shape[0]
    row = lax.broadcasted_iota(jnp.int32, (rows, rows), 0)
    column = lax.broadcasted_iota(jnp.int32, (rows, rows), 1)
    match = jnp.where(row == column, 1.0, 0.0)
    for side, (own, other) in enumerate(((img, txt), (txt, img))):
        weights = scale_ref[0:1, 0:1] * (weigh(own, other, scale_ref) - match)
        dir_ref[side] = jnp.dot(
            weights.astype(jnp.bfloat16), other, preferred_element_type=jnp.float32
        )


def own_visit(scale, half):
    return call(
        own_kernel,
        jax.ShapeDtypeStruct(half.shape, jnp.float32),
        [VMEM, VMEM],
        VMEM,
        name="own",
    )(scale, half)


def gather_side(side, kinds, blocks, others_ref):
    rows, count = blocks[0].shape[0], 0
    for (at, raw), block in zip(kinds, blocks):
        if at == side:
            held = pl.ds(count * rows, rows)
            others_ref[held] = unit_half(block[...]) if raw else block[...]
            count += 1
    return others_ref[pl.ds(0, count * rows)] if count else None


def visit_all(kinds, blocks, scale_ref, half_ref, dir_ref, acc_ref, others_ref, sides=(0, 1)):
    for side in sides:
        others = gather_side(side, kinds, blocks, others_ref) if blocks else None
        if others is None:
            acc_ref[side] = dir_ref[side]
        else:
            acc_ref[side] = dir_ref[side] + visit(half_ref[side], others, scale_ref)
    for (side, raw), block in zip(kinds, blocks):
        if side >= 2:
            at = odd_row() if side == 2 else 1 - odd_row()
            other = unit_half(block[...]) if raw else block[...]
            acc_ref[at] += visit(half_ref[at], other, scale_ref)


def finish(raw_ref, acc_ref, grad_ref, held_ref, sems):
    copies = []
    for n, (start, size) in enumerate(pieces(held_ref.shape[0])):
        at = pl.ds(start, size)
        held_ref[at] = unit_back(raw_ref[at], acc_ref[at])
        copies.append(pltpu.make_async_copy(held_ref.at[at], grad_ref.at[at], sems.at[n]))
        copies[-1].start()
    for copy in copies:
        copy.wait()


def more_kernel(kinds, scale_ref, half_ref, dir_ref, *rest):
    blocks, (out_ref, others_ref) = rest[:-2], rest[-2:]
    visit_all(kinds, blocks, scale_ref, half_ref, dir_ref, out_ref, others_ref)


def image_kernel(kinds, scale_ref, half_ref, dir_ref, raw_ref, *rest):
    blocks, (out_ref, grad_ref, others_ref, held_ref, sems) = rest[:-5], rest[-5:]
    visit_all(kinds, blocks, scale_ref, half_ref, dir_ref, out_ref, others_ref)
    finish(raw_ref.at[0], out_ref.at[0], grad_ref, held_ref, sems)


def text_kernel(kinds, scale_ref, half_ref, dir_ref, raw_ref, *rest):
    blocks, (grad_ref, acc_ref, others_ref, held_ref, sems) = rest[:-5], rest[-5:]
    visit_all(kinds, blocks, scale_ref, half_ref, dir_ref, acc_ref, others_ref, sides=(1,))
    finish(raw_ref.at[1], acc_ref.at[1], grad_ref, held_ref, sems)


def visits(kernel, scale, half, direction, entries, raw=None):
    kinds, blocks = zip(*entries) if entries else ((), ())
    rows, width = half.shape[1:]
    same = jax.ShapeDtypeStruct(direction.shape, direction.dtype)
    grad = jax.ShapeDtypeStruct((rows, width), jnp.float32)
    operands = [scale, half, direction] + ([] if raw is None else [raw])
    most = max([1] + [sum(kind[0] == side for kind in kinds) for side in (0, 1)])
    scratch = [
        pltpu.VMEM((most * rows, width), jnp.bfloat16),
        pltpu.VMEM(grad.shape, grad.dtype),
        pltpu.SemaphoreType.DMA((len(pieces(rows)),)),
    ]
    if kernel is more_kernel:
        out_shape, out_specs, scratch, aliases = same, VMEM, scratch[:1], {2: 0}
    elif kernel is image_kernel:
        out_shape, out_specs, aliases = (same, grad), (VMEM, HBM), {2: 0}
    else:
        out_shape, out_specs, aliases = grad, HBM, {}
        scratch = [pltpu.VMEM(same.shape, same.dtype)] + scratch
    return call(
        functools.partial(kernel, kinds),
        out_shape,
        [VMEM] * (len(operands) + len(blocks)),
        out_specs,
        input_output_aliases=aliases,
        scratch_shapes=scratch,
        name=kernel.__name__,
    )(*operands, *blocks)


def tied(entries, *others):
    blocks, others = lax.optimization_barrier(([block for _, block in entries], others))
    return [(kind, block) for (kind, _), block in zip(entries, blocks)], *others


def on_device(
    picture_encoder_output, caption_encoder_output, softness_factor_exponent, logit_offset_term
):
    img, txt = picture_encoder_output, caption_encoder_output
    row_extent = min(8, lax.axis_size("row") // 2)
    column_extent = min(4, lax.axis_size("col") // 2)
    paired = row_extent % 2 == 0 and lax.axis_size("row") % 2 == 0
    swap = lambda s: s ^ 1
    held = [pltpu.with_memory_space_constraint(a, pltpu.HBM) for a in (img, txt)]
    text_cols, image_cols, text_rows, image_rows, swapped, last = [], [], [], [], [], []
    for k in range(1, column_extent):
        text_cols.append(((0, True), along(txt, "col", lambda s: s + k)))
    text_cols, col_img = tied(text_cols, img)
    for k in range(1, column_extent):
        image_cols.append(((1, True), along(col_img, "col", lambda s: s - k)))
    scale, raw, half, near = norm(
        softness_factor_exponent.reshape(1), logit_offset_term.reshape(1), *held
    )
    direction = own_visit(scale, half)
    if paired:
        reach = row_extent - 1
        far, row_img = lax.optimization_barrier((pick(*held), img))
        far = along(far, "row", lambda s: s + reach if s % 2 else s - reach)
        far = [((2, True), far)]
        for d in range(2, row_extent, 2):
            text_rows.append(((0, True), along(txt, "row", lambda s: s + d)))
            image_rows.append(((1, True), along(row_img, "row", lambda s: s - d)))
        for entries in (text_cols, text_rows):
            if entries:
                direction = visits(more_kernel, scale, half, direction, entries)
        tied_rows, near, direction = tied(text_rows, near, direction)
        swapped.append(((3, False), along(near, "row", swap)))
        for kind, block in tied_rows:
            swapped.append((kind, along(block, "row", swap)))
        for kind, block in tied(image_rows + far)[0][: len(image_rows)]:
            last.append((kind, along(block, "row", swap)))
        middle = image_cols + image_rows + swapped
        direction = visits(more_kernel, scale, half, direction, middle)
    else:
        far = text_cols + image_cols
        for k in range(1, row_extent):
            far.append(((0, True), along(txt, "row", lambda s: s + k)))
            far.append(((1, True), along(img, "row", lambda s: s - k)))

    direction, image_grad = visits(image_kernel, scale, half, direction, far, raw)
    return image_grad, visits(text_kernel, scale, half, direction, last, raw)


def solution(mesh):
    return jax.shard_map(
        on_device,
        mesh=mesh,
        in_specs=(P(("row", "col"), None), P(("row", "col"), None), P(), P()),
        out_specs=(P(("row", "col"), None), P(("row", "col"), None)),
        check_vma=False,
    )
```

```python
import functools

import jax
import jax.numpy as jnp
from jax import lax
from jax.experimental import pallas as pl
from jax.experimental.pallas import tpu as pltpu
from jax.sharding import PartitionSpec as P

eps_norm = 1e-06
VMEM = pl.BlockSpec(memory_space=pltpu.VMEM)
SMEM = pl.BlockSpec(memory_space=pltpu.SMEM)
HBM = pl.BlockSpec(memory_space=pltpu.HBM)
LIMIT = 24 * 2**20
PIECES = 4


def along(value, axis, target):
    count = lax.axis_size(axis)
    pairs = [(source, target(source) % count) for source in range(count)]
    return lax.ppermute(value, axis, pairs)


def inverse_norm(values):
    return lax.rsqrt(jnp.sum(values * values, axis=-1, keepdims=True) + eps_norm)


def unit_half(raw):
    values = raw.astype(jnp.float32)
    return (values * inverse_norm(values)).astype(jnp.bfloat16)


def weigh(own, other, scale_ref):
    scores = lax.dot_general(
        own, other, (((1,), (1,)), ((), ())), preferred_element_type=jnp.float32
    )
    return jax.nn.sigmoid(scale_ref[0:1, 0:1] * scores + scale_ref[1:2, 0:1])


def visit(own, other, scale_ref):
    weights = scale_ref[0:1, 0:1] * weigh(own, other, scale_ref)
    return jnp.dot(weights.astype(jnp.bfloat16), other, preferred_element_type=jnp.float32)


def odd_row():
    return lax.axis_index("row") & 1


def unit_back(raw, direction):
    values = raw.astype(jnp.float32)
    inverse = inverse_norm(values)
    unit = values * inverse
    share = jnp.sum(unit * direction, axis=-1, keepdims=True)
    return inverse * (direction - unit * share)


def pieces(rows):
    if rows % (16 * PIECES):
        return [(0, rows)]
    return [(n * rows // PIECES, rows // PIECES) for n in range(PIECES)]


def call(kernel, out_shape, in_specs, out_specs, **more):
    return pl.pallas_call(
        kernel,
        out_shape=out_shape,
        in_specs=in_specs,
        out_specs=out_specs,
        compiler_params=pltpu.CompilerParams(vmem_limit_bytes=LIMIT),
        cost_estimate=pl.CostEstimate(flops=1000, bytes_accessed=1000, transcendentals=0),
        **more,
    )


def pick_kernel(img_ref, txt_ref, out_ref, sems):
    def copy(source):
        parts = [pl.ds(start, size) for start, size in pieces(out_ref.shape[0])]
        copies = [
            pltpu.make_async_copy(source.at[at], out_ref.at[at], sems.at[n])
            for n, at in enumerate(parts)
        ]
        for one in copies:
            one.start()
        for one in copies:
            one.wait()

    odd = odd_row()

    @pl.when(odd == 1)
    def _():
        copy(txt_ref)

    @pl.when(odd != 1)
    def _():
        copy(img_ref)


def pick(img, txt):
    return call(
        pick_kernel,
        jax.ShapeDtypeStruct(img.shape, img.dtype),
        [HBM, HBM],
        VMEM,
        scratch_shapes=[pltpu.SemaphoreType.DMA((len(pieces(img.shape[0])),))],
        name="pick",
    )(img, txt)


def norm_kernel(
    exponent_ref, offset_ref, img_ref, txt_ref, scale_ref, raw_ref, half_ref, img_half, near_ref, sems
):
    parts = pieces(img_ref.shape[0])
    copies = []
    for side, source in ((0, img_ref), (1, txt_ref)):
        for n, (start, size) in enumerate(parts):
            at = pl.ds(start, size)
            copies.append(
                pltpu.make_async_copy(source.at[at], raw_ref.at[side, at], sems.at[side, n])
            )
    for copy in copies:
        copy.start()
    scale_ref[0:1] = jnp.exp(jnp.full((1, 128), exponent_ref[0], jnp.float32))
    scale_ref[1:2] = jnp.full((1, 128), offset_ref[0], jnp.float32)
    for side in (0, 1):
        for n, (start, size) in enumerate(parts):
            copies[side * len(parts) + n].wait()
            at = pl.ds(start, size)
            half_ref[side, at] = unit_half(raw_ref[side, at])
            if side == 0:
                img_half[at] = half_ref[side, at]
    near_ref[...] = half_ref[1 - odd_row()]


def norm(exponent, offset, img, txt):
    rows, width = img.shape
    one = jax.ShapeDtypeStruct((rows, width), jnp.bfloat16)
    both = jax.ShapeDtypeStruct((2, rows, width), jnp.bfloat16)
    return call(
        norm_kernel,
        (
            jax.ShapeDtypeStruct((8, 128), jnp.float32),
            both,
            both,
            one,
            one,
        ),
        [SMEM, SMEM, HBM, HBM],
        (VMEM,) * 5,
        scratch_shapes=[pltpu.SemaphoreType.DMA((2, len(pieces(rows))))],
        name="norm",
    )(exponent, offset, img, txt)


def own_kernel(scale_ref, half_ref, dir_ref):
    img, txt = half_ref[0], half_ref[1]
    rows = img.shape[0]
    row = lax.broadcasted_iota(jnp.int32, (rows, rows), 0)
    column = lax.broadcasted_iota(jnp.int32, (rows, rows), 1)
    match = jnp.where(row == column, 1.0, 0.0)
    for side, (own, other) in enumerate(((img, txt), (txt, img))):
        weights = scale_ref[0:1, 0:1] * (weigh(own, other, scale_ref) - match)
        dir_ref[side] = jnp.dot(
            weights.astype(jnp.bfloat16), other, preferred_element_type=jnp.float32
        )


def own_visit(scale, half):
    return call(
        own_kernel,
        jax.ShapeDtypeStruct(half.shape, jnp.float32),
        [VMEM, VMEM],
        VMEM,
        name="own",
    )(scale, half)


def visit_all(kinds, blocks, scale_ref, half_ref, dir_ref, acc_ref, others_ref):
    rows = half_ref.shape[1]
    held = [others_ref.at[pl.ds(n * rows, rows)] for n in range(len(kinds))]
    order = sorted(range(len(kinds)), key=lambda n: kinds[n][0])
    for place, n in enumerate(order):
        block = blocks[n][...]
        held[place][...] = unit_half(block) if kinds[n][1] else block
    first = 0
    for side in (0, 1):
        count = sum(kind[0] == side for kind in kinds)
        if count:
            others = others_ref[pl.ds(first * rows, count * rows)]
            acc_ref[side] = dir_ref[side] + visit(half_ref[side], others, scale_ref)
        else:
            acc_ref[side] = dir_ref[side]
        first += count
    for place in range(first, len(kinds)):
        at = odd_row() if kinds[order[place]][0] == 2 else 1 - odd_row()
        acc_ref[at] += visit(half_ref[at], held[place][...], scale_ref)


def more_kernel(kinds, scale_ref, half_ref, dir_ref, *rest):
    blocks, (out_ref, others_ref) = rest[: len(kinds)], rest[len(kinds) :]
    visit_all(kinds, blocks, scale_ref, half_ref, dir_ref, out_ref, others_ref)


def finish(raw_ref, acc_ref, grad_ref, held_ref, sems):
    copies = []
    for n, (start, size) in enumerate(pieces(held_ref.shape[0])):
        at = pl.ds(start, size)
        held_ref[at] = unit_back(raw_ref[at], acc_ref[at])
        copies.append(pltpu.make_async_copy(held_ref.at[at], grad_ref.at[at], sems.at[n]))
        copies[-1].start()
    return copies


def last_kernel(kinds, scale_ref, half_ref, dir_ref, raw_ref, *rest):
    blocks, (img_grad, txt_grad, acc_ref, others_ref, held_ref, sems) = (
        rest[: len(kinds)],
        rest[len(kinds) :],
    )
    visit_all(kinds, blocks, scale_ref, half_ref, dir_ref, acc_ref, others_ref)
    copies = []
    for side, grad_ref in ((0, img_grad), (1, txt_grad)):
        copies += finish(
            raw_ref.at[side], acc_ref.at[side], grad_ref, held_ref.at[side], sems.at[side]
        )
    for copy in copies:
        copy.wait()


def more_visits(scale, half, direction, entries, give=True):
    kinds, blocks = zip(*entries)
    rows, width = half.shape[1:]
    sums = jax.ShapeDtypeStruct(direction.shape, direction.dtype)
    halves = (len(kinds) * rows, width)
    return call(
        functools.partial(more_kernel, kinds),
        (sums, jax.ShapeDtypeStruct(halves, jnp.bfloat16)) if give else sums,
        [VMEM] * (3 + len(blocks)),
        (VMEM, VMEM) if give else VMEM,
        scratch_shapes=[] if give else [pltpu.VMEM(halves, jnp.bfloat16)],
        input_output_aliases={2: 0},
        name="more",
    )(scale, half, direction, *blocks)


def last_visits(scale, half, direction, raw, entries):
    kinds, blocks = zip(*entries) if entries else ((), ())
    rows, width = half.shape[1:]
    grad = jax.ShapeDtypeStruct((rows, width), jnp.float32)
    return call(
        functools.partial(last_kernel, kinds),
        (grad, grad),
        [VMEM] * (4 + len(blocks)),
        (HBM, HBM),
        scratch_shapes=[
            pltpu.VMEM(direction.shape, direction.dtype),
            pltpu.VMEM((max(1, len(kinds)) * rows, width), jnp.bfloat16),
            pltpu.VMEM(direction.shape, direction.dtype),
            pltpu.SemaphoreType.DMA((2, len(pieces(rows)))),
        ],
        name="last",
    )(scale, half, direction, raw, *blocks)


def tied(entries, *others):
    blocks, others = lax.optimization_barrier(([block for _, block in entries], others))
    return [(kind, block) for (kind, _), block in zip(entries, blocks)], *others


def on_device(
    picture_encoder_output, caption_encoder_output, softness_factor_exponent, logit_offset_term
):
    img, txt = picture_encoder_output, caption_encoder_output
    row_extent = min(8, lax.axis_size("row") // 2)
    column_extent = min(4, lax.axis_size("col") // 2)
    paired = row_extent % 2 == 0 and lax.axis_size("row") % 2 == 0
    swap = lambda s: s ^ 1
    held = [pltpu.with_memory_space_constraint(a, pltpu.HBM) for a in (img, txt)]
    text_cols, image_cols, text_rows, image_rows, swapped, last = [], [], [], [], [], []
    for k in range(1, column_extent):
        text_cols.append(((0, True), along(txt, "col", lambda s: s + k)))
    scale, raw, half, img_half, near = norm(
        softness_factor_exponent.reshape(1), logit_offset_term.reshape(1), *held
    )
    for k in range(1, column_extent):
        image_cols.append(((1, False), along(img_half, "col", lambda s: s - k)))
    direction = own_visit(scale, half)
    if not paired:
        for k in range(1, row_extent):
            text_rows.append(((0, True), along(txt, "row", lambda s: s + k)))
            image_rows.append(((1, False), along(img_half, "row", lambda s: s - k)))
        last = text_cols + image_cols + text_rows + image_rows
        return last_visits(scale, half, direction, raw, last)

    reach = row_extent - 1
    far = along(pick(*held), "row", lambda s: s + reach if s % 2 else s - reach)
    for d in range(2, row_extent, 2):
        text_rows.append(((0, True), along(txt, "row", lambda s: s + d)))
        image_rows.append(((1, False), along(img_half, "row", lambda s: s - d)))
    if text_cols:
        direction = more_visits(scale, half, direction, text_cols, False)
    if text_rows:
        direction, halves = more_visits(scale, half, direction, text_rows)
        for n in range(len(text_rows)):
            block = halves[n * img.shape[0] : (n + 1) * img.shape[0]]
            last.append(((0, False), along(block, "row", swap)))
    near, far, direction = lax.optimization_barrier((near, far, direction))
    last.append(((3, False), along(near, "row", swap)))
    for kind, block in image_rows:
        last.append((kind, along(block, "row", swap)))
    if image_rows:
        direction = more_visits(scale, half, direction, image_rows, False)
    direction = more_visits(scale, half, direction, [((2, True), far)] + image_cols, False)
    return last_visits(scale, half, direction, raw, last)


def solution(mesh):
    return jax.shard_map(
        on_device,
        mesh=mesh,
        in_specs=(P(("row", "col"), None), P(("row", "col"), None), P(), P()),
        out_specs=(P(("row", "col"), None), P(("row", "col"), None)),
        check_vma=False,
    )
```

```python
import functools

import jax
import jax.numpy as jnp
from jax import lax
from jax.experimental import pallas as pl
from jax.experimental.pallas import tpu as pltpu
from jax.sharding import PartitionSpec as P

eps_norm = 1e-06
VMEM = pl.BlockSpec(memory_space=pltpu.VMEM)
SMEM = pl.BlockSpec(memory_space=pltpu.SMEM)
HBM = pl.BlockSpec(memory_space=pltpu.HBM)
LIMIT = 24 * 2**20
PIECES = 4
CUTS = 2


def along(value, axis, target):
    count = lax.axis_size(axis)
    pairs = [(source, target(source) % count) for source in range(count)]
    return lax.ppermute(value, axis, pairs)


def inverse_norm(values):
    return lax.rsqrt(jnp.sum(values * values, axis=-1, keepdims=True) + eps_norm)


def unit_half(raw):
    values = raw.astype(jnp.float32)
    return (values * inverse_norm(values)).astype(jnp.bfloat16)


def weigh(own, other, scale_ref):
    scores = lax.dot_general(
        own, other, (((1,), (1,)), ((), ())), preferred_element_type=jnp.float32
    )
    return jax.nn.sigmoid(scale_ref[0:1, 0:1] * scores + scale_ref[1:2, 0:1])


def visit(own, other, scale_ref):
    weights = scale_ref[0:1, 0:1] * weigh(own, other, scale_ref)
    return jnp.dot(weights.astype(jnp.bfloat16), other, preferred_element_type=jnp.float32)


def odd_row():
    return lax.axis_index("row") & 1


def unit_back(raw, direction):
    values = raw.astype(jnp.float32)
    inverse = inverse_norm(values)
    unit = values * inverse
    share = jnp.sum(unit * direction, axis=-1, keepdims=True)
    return inverse * (direction - unit * share)


def pieces(rows, count=PIECES):
    if rows % (16 * count):
        return [(0, rows)]
    return [(n * rows // count, rows // count) for n in range(count)]


def cuts(block):
    return [
        jax.ShapeDtypeStruct((size,) + block.shape[1:], block.dtype)
        for _, size in pieces(block.shape[0], CUTS)
    ]


def call(kernel, out_shape, in_specs, out_specs, **more):
    return pl.pallas_call(
        kernel,
        out_shape=out_shape,
        in_specs=in_specs,
        out_specs=out_specs,
        compiler_params=pltpu.CompilerParams(vmem_limit_bytes=LIMIT),
        cost_estimate=pl.CostEstimate(flops=1000, bytes_accessed=1000, transcendentals=0),
        **more,
    )


def norm_kernel(img_ref, txt_ref, raw_ref, half_ref, img_half, far_ref, *rest):
    near, sems = rest[:-1], rest[-1]
    parts = pieces(img_ref.shape[0])
    copies = []
    for side, source in ((0, img_ref), (1, txt_ref)):
        for n, (start, size) in enumerate(parts):
            at = pl.ds(start, size)
            copies.append(
                pltpu.make_async_copy(source.at[at], raw_ref.at[side, at], sems.at[side, n])
            )
    for copy in copies:
        copy.start()
    for side in (0, 1):
        for n, (start, size) in enumerate(parts):
            copies[side * len(parts) + n].wait()
            at = pl.ds(start, size)
            half_ref[side, at] = unit_half(raw_ref[side, at])
            if side == 0:
                img_half[at] = half_ref[side, at]
    far_ref[...] = half_ref[odd_row()]
    for cut in near:
        cut[...] = half_ref[1 - odd_row()]


def norm(img, txt):
    rows, width = img.shape
    one = jax.ShapeDtypeStruct((rows, width), jnp.bfloat16)
    both = jax.ShapeDtypeStruct((2, rows, width), jnp.bfloat16)
    near = [one]
    return call(
        norm_kernel,
        (both, both, one, one, *near),
        [HBM, HBM],
        (VMEM,) * (4 + len(near)),
        scratch_shapes=[pltpu.SemaphoreType.DMA((2, len(pieces(rows))))],
        name="norm",
    )(img, txt)


def own_kernel(exponent_ref, offset_ref, half_ref, scale_ref, dir_ref):
    scale_ref[0:1] = jnp.exp(jnp.full((1, 128), exponent_ref[0], jnp.float32))
    scale_ref[1:2] = jnp.full((1, 128), offset_ref[0], jnp.float32)
    img, txt = half_ref[0], half_ref[1]
    rows = img.shape[0]
    row = lax.broadcasted_iota(jnp.int32, (rows, rows), 0)
    column = lax.broadcasted_iota(jnp.int32, (rows, rows), 1)
    match = jnp.where(row == column, 1.0, 0.0)
    for side, (own, other) in enumerate(((img, txt), (txt, img))):
        weights = scale_ref[0:1, 0:1] * (weigh(own, other, scale_ref) - match)
        dir_ref[side] = jnp.dot(
            weights.astype(jnp.bfloat16), other, preferred_element_type=jnp.float32
        )


def own_visit(exponent, offset, half):
    return call(
        own_kernel,
        (
            jax.ShapeDtypeStruct((8, 128), jnp.float32),
            jax.ShapeDtypeStruct(half.shape, jnp.float32),
        ),
        [SMEM, SMEM, VMEM],
        (VMEM, VMEM),
        name="own",
    )(exponent.reshape(1), offset.reshape(1), half)


def parts_of(kinds, refs, rows):
    refs, blocks = list(refs), []
    for _ in kinds:
        block = [refs.pop(0)]
        while sum(part.shape[0] for part in block) < rows:
            block.append(refs.pop(0))
        blocks.append(block)
    return blocks


def flat(entries):
    kinds = tuple(kind for kind, _ in entries)
    return kinds, jax.tree.leaves([block for _, block in entries])


def visit_all(kinds, blocks, scale_ref, half_ref, dir_ref, acc_ref, others_ref):
    rows = half_ref.shape[1]
    blocks = parts_of(kinds, blocks, rows)
    held = [others_ref.at[pl.ds(n * rows, rows)] for n in range(len(kinds))]
    order = sorted(range(len(kinds)), key=lambda n: kinds[n][0])
    for place, n in enumerate(order):
        start = 0
        for part in blocks[n]:
            if kinds[n][0] == 4:
                held[place][...] = part[pl.ds(pl.multiple_of((1 - odd_row()) * rows, 16), rows)]
                continue
            size = part.shape[0]
            block = part[...]
            held[place][pl.ds(start, size)] = unit_half(block) if kinds[n][1] else block
            start += size
    first = 0
    for side in (0, 1):
        count = sum(kind[0] == side for kind in kinds)
        if count:
            others = others_ref[pl.ds(first * rows, count * rows)]
            acc_ref[side] = dir_ref[side] + visit(half_ref[side], others, scale_ref)
        else:
            acc_ref[side] = dir_ref[side]
        first += count
    for place in range(first, len(kinds)):
        at = odd_row() if kinds[order[place]][0] == 2 else 1 - odd_row()
        acc_ref[at] += visit(half_ref[at], held[place][...], scale_ref)


def more_kernel(kinds, given, scale_ref, half_ref, dir_ref, *rest):
    blocks, rest = rest[: len(rest) - 2 - given], rest[len(rest) - 2 - given :]
    out_ref, halves, others_ref = rest[0], rest[1:-1], rest[-1]
    visit_all(kinds, blocks, scale_ref, half_ref, dir_ref, out_ref, others_ref)
    start = 0
    for cut in halves:
        cut[...] = others_ref[pl.ds(start, cut.shape[0])]
        start += cut.shape[0]


def finish(raw_ref, acc_ref, grad_ref, held_ref, sems):
    copies = []
    for n, (start, size) in enumerate(pieces(held_ref.shape[0])):
        at = pl.ds(start, size)
        held_ref[at] = unit_back(raw_ref[at], acc_ref[at])
        copies.append(pltpu.make_async_copy(held_ref.at[at], grad_ref.at[at], sems.at[n]))
        copies[-1].start()
    return copies


def last_kernel(kinds, sides, scale_ref, half_ref, dir_ref, raw_ref, *rest):
    blocks, grads = rest[: -4 - len(sides)], rest[-4 - len(sides) : -4]
    acc_ref, others_ref, held_ref, sems = rest[-4:]
    visit_all(kinds, blocks, scale_ref, half_ref, dir_ref, acc_ref, others_ref)
    copies = []
    for side, grad_ref in zip(sides, grads):
        copies += finish(
            raw_ref.at[side], acc_ref.at[side], grad_ref, held_ref.at[side], sems.at[side]
        )
    for copy in copies:
        copy.wait()


def image_kernel(kinds, scale_ref, half_ref, dir_ref, raw_ref, *rest):
    blocks, (out_ref, grad_ref, others_ref, held_ref, sems) = rest[:-5], rest[-5:]
    visit_all(kinds, blocks, scale_ref, half_ref, dir_ref, out_ref, others_ref)
    for copy in finish(raw_ref.at[0], out_ref.at[0], grad_ref, held_ref, sems):
        copy.wait()


def more_visits(scale, half, direction, entries, give=False):
    kinds, blocks = flat(entries)
    rows, width = half.shape[1:]
    one = jax.ShapeDtypeStruct((rows, width), jnp.bfloat16)
    halves = cuts(one) * sum(side == 0 for side, _ in kinds) if give else []
    direction, *halves = call(
        functools.partial(more_kernel, kinds, len(halves)),
        (jax.ShapeDtypeStruct(direction.shape, direction.dtype), *halves),
        [VMEM] * (3 + len(blocks)),
        (VMEM,) * (1 + len(halves)),
        scratch_shapes=[pltpu.VMEM((len(kinds) * rows, width), jnp.bfloat16)],
        input_output_aliases={2: 0},
        name="more",
    )(scale, half, direction, *blocks)
    return (direction, halves) if give else direction


def image_visits(scale, half, direction, raw, entries):
    kinds, blocks = flat(entries)
    rows, width = half.shape[1:]
    grad = jax.ShapeDtypeStruct((rows, width), jnp.float32)
    return call(
        functools.partial(image_kernel, kinds),
        (jax.ShapeDtypeStruct(direction.shape, direction.dtype), grad),
        [VMEM] * (4 + len(blocks)),
        (VMEM, HBM),
        scratch_shapes=[
            pltpu.VMEM((len(kinds) * rows, width), jnp.bfloat16),
            pltpu.VMEM(grad.shape, grad.dtype),
            pltpu.SemaphoreType.DMA((len(pieces(rows)),)),
        ],
        input_output_aliases={2: 0},
        name="image",
    )(scale, half, direction, raw, *blocks)


def last_visits(scale, half, direction, raw, entries, sides):
    kinds, blocks = flat(entries)
    rows, width = half.shape[1:]
    grad = jax.ShapeDtypeStruct((rows, width), jnp.float32)
    return call(
        functools.partial(last_kernel, kinds, sides),
        (grad,) * len(sides),
        [VMEM] * (4 + len(blocks)),
        (HBM,) * len(sides),
        scratch_shapes=[
            pltpu.VMEM(direction.shape, direction.dtype),
            pltpu.VMEM((max(1, len(kinds)) * rows, width), jnp.bfloat16),
            pltpu.VMEM(direction.shape, direction.dtype),
            pltpu.SemaphoreType.DMA((2, len(pieces(rows)))),
        ],
        name="last",
    )(scale, half, direction, raw, *blocks)


def tied(entries, *others):
    blocks, others = lax.optimization_barrier(([block for _, block in entries], others))
    return [(kind, block) for (kind, _), block in zip(entries, blocks)], *others


def on_device(
    picture_encoder_output, caption_encoder_output, softness_factor_exponent, logit_offset_term
):
    img, txt = picture_encoder_output, caption_encoder_output
    row_extent = min(8, lax.axis_size("row") // 2)
    column_extent = min(4, lax.axis_size("col") // 2)
    paired = row_extent % 2 == 0 and lax.axis_size("row") % 2 == 0
    swap = lambda s: s ^ 1
    held = [pltpu.with_memory_space_constraint(a, pltpu.HBM) for a in (img, txt)]
    text_cols, image_cols, text_rows, image_rows, swapped, last = [], [], [], [], [], []
    for k in range(1, column_extent):
        text_cols.append(((0, True), along(txt, "col", lambda s: s + k)))
    raw, half, img_half, far, *near = norm(*held)
    for k in range(1, column_extent):
        image_cols.append(((1, False), along(img_half, "col", lambda s: s - k)))
    scale, direction = own_visit(softness_factor_exponent, logit_offset_term, half)
    if not paired:
        for k in range(1, row_extent):
            text_rows.append(((0, True), along(txt, "row", lambda s: s + k)))
            image_rows.append(((1, False), along(img_half, "row", lambda s: s - k)))
        last = text_cols + image_cols + text_rows + image_rows
        return last_visits(scale, half, direction, raw, last, (0, 1))

    reach = row_extent - 1
    far = along(far, "row", lambda s: s + reach if s % 2 else s - reach)
    for d in range(2, row_extent, 2):
        text_rows.append(((0, True), along(txt, "row", lambda s: s + d)))
        image_rows.append(((1, False), along(img_half, "row", lambda s: s - d)))
    groups = [[n, n + 1] for n in range(0, lax.axis_size("row"), 2)]
    near = lax.all_gather(near[0], "row", axis_index_groups=groups, tiled=True)
    near = ((4, False), near)
    if text_cols:
        direction = more_visits(scale, half, direction, text_cols)
    if text_rows:
        direction, halves = more_visits(scale, half, direction, text_rows, give=True)
        per = len(halves) // len(text_rows)
        for n in range(len(text_rows)):
            block = halves[n * per : (n + 1) * per]
            swapped.append(((0, False), [along(cut, "row", swap) for cut in block]))
    direction = more_visits(scale, half, direction, swapped + [near])
    far = [((2, False), far)]
    middle, direction = tied(image_rows + image_cols + far, direction)
    for kind, block in middle[: len(image_rows)]:
        last.append((kind, along(block, "row", swap)))
    direction, image_grad = image_visits(scale, half, direction, raw, middle)
    (text_grad,) = last_visits(scale, half, direction, raw, last, (1,))
    return image_grad, text_grad


def solution(mesh):
    return jax.shard_map(
        on_device,
        mesh=mesh,
        in_specs=(P(("row", "col"), None), P(("row", "col"), None), P(), P()),
        out_specs=(P(("row", "col"), None), P(("row", "col"), None)),
        check_vma=False,
    )
```

```python
import functools

import jax
import jax.numpy as jnp
from jax import lax
from jax.experimental import pallas as pl
from jax.experimental.pallas import tpu as pltpu
from jax.sharding import PartitionSpec as P

eps_norm = 1e-06
VMEM = pl.BlockSpec(memory_space=pltpu.VMEM)
SMEM = pl.BlockSpec(memory_space=pltpu.SMEM)
HBM = pl.BlockSpec(memory_space=pltpu.HBM)
LIMIT = 24 * 2**20
PIECES = 4


def along(value, axis, target):
    count = lax.axis_size(axis)
    pairs = [(source, target(source) % count) for source in range(count)]
    return lax.ppermute(value, axis, pairs)


def inverse_norm(values):
    return lax.rsqrt(jnp.sum(values * values, axis=-1, keepdims=True) + eps_norm)


def unit_half(raw):
    values = raw.astype(jnp.float32)
    return (values * inverse_norm(values)).astype(jnp.bfloat16)


def weigh(own, other, scale_ref):
    scores = lax.dot_general(
        own, other, (((1,), (1,)), ((), ())), preferred_element_type=jnp.float32
    )
    return jax.nn.sigmoid(scale_ref[0:1, 0:1] * scores + scale_ref[1:2, 0:1])


def visit(own, other, scale_ref):
    weights = scale_ref[0:1, 0:1] * weigh(own, other, scale_ref)
    return jnp.dot(weights.astype(jnp.bfloat16), other, preferred_element_type=jnp.float32)


def odd_row():
    return lax.axis_index("row") & 1


def unit_back(raw, direction):
    values = raw.astype(jnp.float32)
    inverse = inverse_norm(values)
    unit = values * inverse
    share = jnp.sum(unit * direction, axis=-1, keepdims=True)
    return inverse * (direction - unit * share)


def pieces(rows, count=PIECES):
    if rows % (16 * count):
        return [(0, rows)]
    return [(n * rows // count, rows // count) for n in range(count)]


def call(kernel, out_shape, in_specs, out_specs, **more):
    return pl.pallas_call(
        kernel,
        out_shape=out_shape,
        in_specs=in_specs,
        out_specs=out_specs,
        compiler_params=pltpu.CompilerParams(vmem_limit_bytes=LIMIT),
        cost_estimate=pl.CostEstimate(flops=1000, bytes_accessed=1000, transcendentals=0),
        **more,
    )


def pick_kernel(img_ref, txt_ref, out_ref, sems):
    def copy(source):
        parts = [pl.ds(start, size) for start, size in pieces(out_ref.shape[0])]
        copies = [
            pltpu.make_async_copy(source.at[at], out_ref.at[at], sems.at[n])
            for n, at in enumerate(parts)
        ]
        for one in copies:
            one.start()
        for one in copies:
            one.wait()

    odd = odd_row()

    @pl.when(odd == 1)
    def _():
        copy(txt_ref)

    @pl.when(odd != 1)
    def _():
        copy(img_ref)


def pick(img, txt):
    return call(
        pick_kernel,
        jax.ShapeDtypeStruct(img.shape, img.dtype),
        [HBM, HBM],
        VMEM,
        scratch_shapes=[pltpu.SemaphoreType.DMA((len(pieces(img.shape[0])),))],
        name="pick",
    )(img, txt)


def norm_kernel(img_ref, txt_ref, raw_ref, half_ref, img_half, sems):
    parts = pieces(img_ref.shape[0])
    copies = []
    for side, source in ((0, img_ref), (1, txt_ref)):
        for n, (start, size) in enumerate(parts):
            at = pl.ds(start, size)
            copies.append(
                pltpu.make_async_copy(source.at[at], raw_ref.at[side, at], sems.at[side, n])
            )
    for copy in copies:
        copy.start()
    for side in (0, 1):
        for n, (start, size) in enumerate(parts):
            copies[side * len(parts) + n].wait()
            at = pl.ds(start, size)
            half_ref[side, at] = unit_half(raw_ref[side, at])
            if side == 0:
                img_half[at] = half_ref[side, at]


def norm(img, txt):
    rows, width = img.shape
    one = jax.ShapeDtypeStruct((rows, width), jnp.bfloat16)
    both = jax.ShapeDtypeStruct((2, rows, width), jnp.bfloat16)
    return call(
        norm_kernel,
        (both, both, one),
        [HBM, HBM],
        (VMEM,) * 3,
        scratch_shapes=[pltpu.SemaphoreType.DMA((2, len(pieces(rows))))],
        name="norm",
    )(img, txt)


def own_kernel(exponent_ref, offset_ref, half_ref, scale_ref, dir_ref):
    scale_ref[0:1] = jnp.exp(jnp.full((1, 128), exponent_ref[0], jnp.float32))
    scale_ref[1:2] = jnp.full((1, 128), offset_ref[0], jnp.float32)
    img, txt = half_ref[0], half_ref[1]
    rows = img.shape[0]
    row = lax.broadcasted_iota(jnp.int32, (rows, rows), 0)
    column = lax.broadcasted_iota(jnp.int32, (rows, rows), 1)
    match = jnp.where(row == column, 1.0, 0.0)
    for side, (own, other) in enumerate(((img, txt), (txt, img))):
        weights = scale_ref[0:1, 0:1] * (weigh(own, other, scale_ref) - match)
        dir_ref[side] = jnp.dot(
            weights.astype(jnp.bfloat16), other, preferred_element_type=jnp.float32
        )


def own_visit(exponent, offset, half):
    return call(
        own_kernel,
        (
            jax.ShapeDtypeStruct((8, 128), jnp.float32),
            jax.ShapeDtypeStruct(half.shape, jnp.float32),
        ),
        [SMEM, SMEM, VMEM],
        (VMEM, VMEM),
        name="own",
    )(exponent.reshape(1), offset.reshape(1), half)


def flat(entries):
    return tuple(kind for kind, _ in entries), [block for _, block in entries]


def visit_all(kinds, blocks, scale_ref, half_ref, dir_ref, acc_ref, others_ref):
    rows = half_ref.shape[1]
    held = [others_ref.at[pl.ds(n * rows, rows)] for n in range(len(kinds))]
    order = sorted(range(len(kinds)), key=lambda n: kinds[n][0])
    for place, n in enumerate(order):
        block = blocks[n][...]
        held[place][...] = unit_half(block) if kinds[n][1] else block
    first = 0
    for side in (0, 1):
        count = sum(kind[0] == side for kind in kinds)
        if count:
            others = others_ref[pl.ds(first * rows, count * rows)]
            acc_ref[side] = dir_ref[side] + visit(half_ref[side], others, scale_ref)
        else:
            acc_ref[side] = dir_ref[side]
        first += count
    for place in range(first, len(kinds)):
        at = odd_row() if kinds[order[place]][0] == 2 else 1 - odd_row()
        acc_ref[at] += visit(half_ref[at], held[place][...], scale_ref)


def more_kernel(kinds, give, scale_ref, half_ref, dir_ref, *rest):
    blocks, rest = rest[: len(kinds)], rest[len(kinds) :]
    out_ref, others_ref = rest[0], rest[-1]
    visit_all(kinds, blocks, scale_ref, half_ref, dir_ref, out_ref, others_ref)
    if give:
        rows, count = half_ref.shape[1], len(kinds)
        to = 1 - odd_row()
        if kinds:
            rest[1][to, pl.ds(0, count * rows)] = others_ref[...]
        rest[1][to, pl.ds(count * rows, rows)] = half_ref[to]


def pair_kernel(scale_ref, half_ref, dir_ref, both_ref, out_ref):
    rows, at = half_ref.shape[1], 1 - odd_row()
    held = both_ref.at[at]
    count = both_ref.shape[1] - rows
    out_ref[1] = dir_ref[1]
    if count:
        out_ref[0] = dir_ref[0] + visit(half_ref[0], held[pl.ds(0, count)], scale_ref)
    else:
        out_ref[0] = dir_ref[0]
    out_ref[at] += visit(half_ref[at], held[pl.ds(count, rows)], scale_ref)


def finish(raw_ref, acc_ref, grad_ref, held_ref, sems):
    copies = []
    for n, (start, size) in enumerate(pieces(held_ref.shape[0])):
        at = pl.ds(start, size)
        held_ref[at] = unit_back(raw_ref[at], acc_ref[at])
        copies.append(pltpu.make_async_copy(held_ref.at[at], grad_ref.at[at], sems.at[n]))
        copies[-1].start()
    return copies


def last_kernel(kinds, sides, scale_ref, half_ref, dir_ref, raw_ref, *rest):
    blocks, grads = rest[: -4 - len(sides)], rest[-4 - len(sides) : -4]
    acc_ref, others_ref, held_ref, sems = rest[-4:]
    visit_all(kinds, blocks, scale_ref, half_ref, dir_ref, acc_ref, others_ref)
    copies = []
    for side, grad_ref in zip(sides, grads):
        copies += finish(
            raw_ref.at[side], acc_ref.at[side], grad_ref, held_ref.at[side], sems.at[side]
        )
    for copy in copies:
        copy.wait()


def image_kernel(kinds, scale_ref, half_ref, dir_ref, raw_ref, *rest):
    blocks, (out_ref, grad_ref, others_ref, held_ref, sems) = rest[:-5], rest[-5:]
    visit_all(kinds, blocks, scale_ref, half_ref, dir_ref, out_ref, others_ref)
    for copy in finish(raw_ref.at[0], out_ref.at[0], grad_ref, held_ref, sems):
        copy.wait()


def more_visits(scale, half, direction, entries, give=False):
    kinds, blocks = flat(entries)
    rows, width = half.shape[1:]
    sums = jax.ShapeDtypeStruct(direction.shape, direction.dtype)
    pair = jax.ShapeDtypeStruct((2, (len(kinds) + 1) * rows, width), jnp.bfloat16)
    return call(
        functools.partial(more_kernel, kinds, give),
        (sums, pair) if give else sums,
        [VMEM] * (3 + len(blocks)),
        (VMEM, VMEM) if give else VMEM,
        scratch_shapes=[pltpu.VMEM((max(1, len(kinds)) * rows, width), jnp.bfloat16)],
        input_output_aliases={2: 0},
        name="more",
    )(scale, half, direction, *blocks)


def pair_visits(scale, half, direction, both):
    return call(
        pair_kernel,
        jax.ShapeDtypeStruct(direction.shape, direction.dtype),
        [VMEM] * 4,
        VMEM,
        input_output_aliases={2: 0},
        name="pair",
    )(scale, half, direction, both)


def unit_kernel(raw_ref, half_ref):
    half_ref[...] = unit_half(raw_ref[...])


def normalized(raw):
    return call(unit_kernel, jax.ShapeDtypeStruct(raw.shape, raw.dtype), [VMEM], VMEM, name="unit")(raw)


def image_visits(scale, half, direction, raw, entries):
    kinds, blocks = flat(entries)
    rows, width = half.shape[1:]
    grad = jax.ShapeDtypeStruct((rows, width), jnp.float32)
    return call(
        functools.partial(image_kernel, kinds),
        (jax.ShapeDtypeStruct(direction.shape, direction.dtype), grad),
        [VMEM] * (4 + len(blocks)),
        (VMEM, HBM),
        scratch_shapes=[
            pltpu.VMEM((len(kinds) * rows, width), jnp.bfloat16),
            pltpu.VMEM(grad.shape, grad.dtype),
            pltpu.SemaphoreType.DMA((len(pieces(rows)),)),
        ],
        input_output_aliases={2: 0},
        name="image",
    )(scale, half, direction, raw, *blocks)


def last_visits(scale, half, direction, raw, entries, sides):
    kinds, blocks = flat(entries)
    rows, width = half.shape[1:]
    grad = jax.ShapeDtypeStruct((rows, width), jnp.float32)
    return call(
        functools.partial(last_kernel, kinds, sides),
        (grad,) * len(sides),
        [VMEM] * (4 + len(blocks)),
        (HBM,) * len(sides),
        scratch_shapes=[
            pltpu.VMEM(direction.shape, direction.dtype),
            pltpu.VMEM((max(1, len(kinds)) * rows, width), jnp.bfloat16),
            pltpu.VMEM(direction.shape, direction.dtype),
            pltpu.SemaphoreType.DMA((2, len(pieces(rows)))),
        ],
        name="last",
    )(scale, half, direction, raw, *blocks)


def tied(entries, *others):
    blocks, others = lax.optimization_barrier(([block for _, block in entries], others))
    return [(kind, block) for (kind, _), block in zip(entries, blocks)], *others


def on_device(
    picture_encoder_output, caption_encoder_output, softness_factor_exponent, logit_offset_term
):
    img, txt = picture_encoder_output, caption_encoder_output
    row_extent = min(8, lax.axis_size("row") // 2)
    column_extent = min(4, lax.axis_size("col") // 2)
    paired = row_extent % 2 == 0 and lax.axis_size("row") % 2 == 0
    swap = lambda s: s ^ 1
    held = [pltpu.with_memory_space_constraint(a, pltpu.HBM) for a in (img, txt)]
    text_cols, image_cols, text_rows, image_rows, last = [], [], [], [], []
    for k in range(1, column_extent):
        text_cols.append(((0, True), along(txt, "col", lambda s: s + k)))
    raw, half, img_half = norm(*held)
    for k in range(1, column_extent):
        image_cols.append(((1, False), along(img_half, "col", lambda s: s - k)))
    scale, direction = own_visit(softness_factor_exponent, logit_offset_term, half)
    if not paired:
        for k in range(1, row_extent):
            text_rows.append(((0, True), along(txt, "row", lambda s: s + k)))
            image_rows.append(((1, False), along(img_half, "row", lambda s: s - k)))
        last = text_cols + image_cols + text_rows + image_rows
        return last_visits(scale, half, direction, raw, last, (0, 1))

    reach = row_extent - 1
    far = along(pick(*held), "row", lambda s: s + reach if s % 2 else s - reach)
    for d in range(2, row_extent, 2):
        text_rows.append(((0, True), along(txt, "row", lambda s: s + d)))
        image_rows.append(((1, False), along(img_half, "row", lambda s: s - d)))
    if text_cols:
        direction = more_visits(scale, half, direction, text_cols)
    direction, both = more_visits(scale, half, direction, text_rows, give=True)
    groups = [[n, n + 1] for n in range(0, lax.axis_size("row"), 2)]
    both = lax.all_to_all(both, "row", 0, 0, axis_index_groups=groups)
    direction = pair_visits(scale, half, direction, both)
    far = [((2, False), normalized(far))]
    middle, direction = tied(image_rows + image_cols + far, direction)
    for kind, block in middle[: len(image_rows)]:
        last.append((kind, along(block, "row", swap)))
    direction, image_grad = image_visits(scale, half, direction, raw, middle)
    (text_grad,) = last_visits(scale, half, direction, raw, last, (1,))
    return image_grad, text_grad


def solution(mesh):
    return jax.shard_map(
        on_device,
        mesh=mesh,
        in_specs=(P(("row", "col"), None), P(("row", "col"), None), P(), P()),
        out_specs=(P(("row", "col"), None), P(("row", "col"), None)),
        check_vma=False,
    )
```

```python
import functools

import jax
import jax.numpy as jnp
from jax import lax
from jax.experimental import pallas as pl
from jax.experimental.pallas import tpu as pltpu
from jax.sharding import PartitionSpec as P

eps_norm = 1e-06
VMEM = pl.BlockSpec(memory_space=pltpu.VMEM)
SMEM = pl.BlockSpec(memory_space=pltpu.SMEM)
HBM = pl.BlockSpec(memory_space=pltpu.HBM)
LIMIT = 24 * 2**20
PIECES = 4
CUTS = 2


def along(value, axis, target):
    count = lax.axis_size(axis)
    pairs = [(source, target(source) % count) for source in range(count)]
    return lax.ppermute(value, axis, pairs)


def inverse_norm(values):
    return lax.rsqrt(jnp.sum(values * values, axis=-1, keepdims=True) + eps_norm)


def unit_half(raw):
    values = raw.astype(jnp.float32)
    return (values * inverse_norm(values)).astype(jnp.bfloat16)


def weigh(own, other, scale_ref):
    scores = lax.dot_general(
        own, other, (((1,), (1,)), ((), ())), preferred_element_type=jnp.float32
    )
    return jax.nn.sigmoid(scale_ref[0:1, 0:1] * scores + scale_ref[1:2, 0:1])


def visit(own, other, scale_ref):
    weights = scale_ref[0:1, 0:1] * weigh(own, other, scale_ref)
    return jnp.dot(weights.astype(jnp.bfloat16), other, preferred_element_type=jnp.float32)


def odd_row():
    return lax.axis_index("row") & 1


def unit_back(raw, direction):
    values = raw.astype(jnp.float32)
    inverse = inverse_norm(values)
    unit = values * inverse
    share = jnp.sum(unit * direction, axis=-1, keepdims=True)
    return inverse * (direction - unit * share)


def pieces(rows, count=PIECES):
    if rows % (16 * count):
        return [(0, rows)]
    return [(n * rows // count, rows // count) for n in range(count)]


def cuts(block):
    return [
        jax.ShapeDtypeStruct((size,) + block.shape[1:], block.dtype)
        for _, size in pieces(block.shape[0], CUTS)
    ]


def call(kernel, out_shape, in_specs, out_specs, **more):
    return pl.pallas_call(
        kernel,
        out_shape=out_shape,
        in_specs=in_specs,
        out_specs=out_specs,
        compiler_params=pltpu.CompilerParams(vmem_limit_bytes=LIMIT),
        cost_estimate=pl.CostEstimate(flops=1000, bytes_accessed=1000, transcendentals=0),
        **more,
    )


def pick_kernel(img_ref, txt_ref, out_ref, sems):
    def copy(source):
        parts = [pl.ds(start, size) for start, size in pieces(out_ref.shape[0])]
        copies = [
            pltpu.make_async_copy(source.at[at], out_ref.at[at], sems.at[n])
            for n, at in enumerate(parts)
        ]
        for one in copies:
            one.start()
        for one in copies:
            one.wait()

    odd = odd_row()

    @pl.when(odd == 1)
    def _():
        copy(txt_ref)

    @pl.when(odd != 1)
    def _():
        copy(img_ref)


def pick(img, txt):
    return call(
        pick_kernel,
        jax.ShapeDtypeStruct(img.shape, img.dtype),
        [HBM, HBM],
        VMEM,
        scratch_shapes=[pltpu.SemaphoreType.DMA((len(pieces(img.shape[0])),))],
        name="pick",
    )(img, txt)


def load(sources, raw_refs, sems):
    parts = pieces(sources[0].shape[0])
    started = []
    for side, (source, raw_ref) in enumerate(zip(sources, raw_refs)):
        started.append([])
        for n, (start, size) in enumerate(parts):
            at = pl.ds(start, size)
            copy = pltpu.make_async_copy(source.at[at], raw_ref.at[at], sems.at[side, n])
            copy.start()
            started[-1].append((at, copy))
    return started


def norm_kernel(img_ref, txt_ref, img_half, txt_half, raw_ref, sems):
    halves = (img_half, txt_half)
    started = load((img_ref, txt_ref), (raw_ref.at[0], raw_ref.at[1]), sems)
    for side, copies in enumerate(started):
        for at, copy in copies:
            copy.wait()
            halves[side][at] = unit_half(raw_ref[side, at])


def norm(img, txt):
    rows, width = img.shape
    one = jax.ShapeDtypeStruct((rows, width), jnp.bfloat16)
    return call(
        norm_kernel,
        (one, one),
        [HBM, HBM],
        (VMEM, VMEM),
        scratch_shapes=[
            pltpu.VMEM((2, rows, width), jnp.bfloat16),
            pltpu.SemaphoreType.DMA((2, len(pieces(rows)))),
        ],
        name="norm",
    )(img, txt)


def own_kernel(
    exponent_ref, offset_ref, img_ref, txt_ref, img_half, txt_half,
    scale_ref, raw_ref, half_ref, near_ref, dir_ref, sems,
):
    started = load((img_ref, txt_ref), (raw_ref.at[0], raw_ref.at[1]), sems)
    scale_ref[0:1] = jnp.exp(jnp.broadcast_to(exponent_ref[...], (1, 128)))
    scale_ref[1:2] = jnp.broadcast_to(offset_ref[...], (1, 128))
    half_ref[0] = img_half[...]
    half_ref[1] = txt_half[...]
    near_ref[...] = half_ref[1 - odd_row()]
    img, txt = half_ref[0], half_ref[1]
    rows = img.shape[0]
    row = lax.broadcasted_iota(jnp.int32, (rows, rows), 0)
    column = lax.broadcasted_iota(jnp.int32, (rows, rows), 1)
    match = jnp.where(row == column, 1.0, 0.0)
    for side, (own, other) in enumerate(((img, txt), (txt, img))):
        weights = scale_ref[0:1, 0:1] * (weigh(own, other, scale_ref) - match)
        dir_ref[side] = jnp.dot(
            weights.astype(jnp.bfloat16), other, preferred_element_type=jnp.float32
        )
    for copies in started:
        for _, copy in copies:
            copy.wait()


def own_visit(exponent, offset, img, txt, img_half, txt_half):
    rows, width = img.shape
    both = jax.ShapeDtypeStruct((2, rows, width), jnp.bfloat16)
    return call(
        own_kernel,
        (
            jax.ShapeDtypeStruct((8, 128), jnp.float32),
            both,
            both,
            jax.ShapeDtypeStruct((rows, width), jnp.bfloat16),
            jax.ShapeDtypeStruct((2, rows, width), jnp.float32),
        ),
        [VMEM, VMEM, HBM, HBM, VMEM, VMEM],
        (VMEM,) * 5,
        scratch_shapes=[pltpu.SemaphoreType.DMA((2, len(pieces(rows))))],
        name="own",
    )(exponent.reshape(1, 1), offset.reshape(1, 1), img, txt, img_half, txt_half)


def parts_of(kinds, refs, rows):
    refs, blocks = list(refs), []
    for _ in kinds:
        block = [refs.pop(0)]
        while sum(part.shape[0] for part in block) < rows:
            block.append(refs.pop(0))
        blocks.append(block)
    return blocks


def flat(entries):
    kinds = tuple(kind for kind, _ in entries)
    return kinds, jax.tree.leaves([block for _, block in entries])


def visit_all(kinds, blocks, scale_ref, half_ref, dir_ref, acc_ref, others_ref):
    rows = half_ref.shape[1]
    blocks = parts_of(kinds, blocks, rows)
    held = [others_ref.at[pl.ds(n * rows, rows)] for n in range(len(kinds))]
    order = sorted(range(len(kinds)), key=lambda n: kinds[n][0])
    for place, n in enumerate(order):
        start = 0
        for part in blocks[n]:
            size = part.shape[0]
            block = part[...]
            held[place][pl.ds(start, size)] = unit_half(block) if kinds[n][1] else block
            start += size
    first = 0
    for side in (0, 1):
        count = sum(kind[0] == side for kind in kinds)
        if count:
            others = others_ref[pl.ds(first * rows, count * rows)]
            acc_ref[side] = dir_ref[side] + visit(half_ref[side], others, scale_ref)
        else:
            acc_ref[side] = dir_ref[side]
        first += count
    for place in range(first, len(kinds)):
        at = odd_row() if kinds[order[place]][0] == 2 else 1 - odd_row()
        acc_ref[at] += visit(half_ref[at], held[place][...], scale_ref)


def more_kernel(kinds, given, scale_ref, half_ref, dir_ref, *rest):
    blocks, rest = rest[: len(rest) - 2 - given], rest[len(rest) - 2 - given :]
    out_ref, halves, others_ref = rest[0], rest[1:-1], rest[-1]
    visit_all(kinds, blocks, scale_ref, half_ref, dir_ref, out_ref, others_ref)
    start = 0
    for cut in halves:
        cut[...] = others_ref[pl.ds(start, cut.shape[0])]
        start += cut.shape[0]


def finish(raw_ref, acc_ref, grad_ref, held_ref, sems):
    copies = []
    for n, (start, size) in enumerate(pieces(held_ref.shape[0])):
        at = pl.ds(start, size)
        held_ref[at] = unit_back(raw_ref[at], acc_ref[at])
        copies.append(pltpu.make_async_copy(held_ref.at[at], grad_ref.at[at], sems.at[n]))
        copies[-1].start()
    return copies


def last_kernel(kinds, scale_ref, half_ref, dir_ref, raw_ref, *rest):
    blocks, (img_grad, txt_grad, acc_ref, others_ref, held_ref, sems) = rest[:-6], rest[-6:]
    visit_all(kinds, blocks, scale_ref, half_ref, dir_ref, acc_ref, others_ref)
    copies = []
    for side, grad_ref in ((0, img_grad), (1, txt_grad)):
        copies += finish(
            raw_ref.at[side], acc_ref.at[side], grad_ref, held_ref.at[side], sems.at[side]
        )
    for copy in copies:
        copy.wait()


def more_visits(scale, half, direction, entries, give=False):
    kinds, blocks = flat(entries)
    rows, width = half.shape[1:]
    one = jax.ShapeDtypeStruct((rows, width), jnp.bfloat16)
    halves = cuts(one) * len(kinds) if give else []
    direction, *halves = call(
        functools.partial(more_kernel, kinds, len(halves)),
        (jax.ShapeDtypeStruct(direction.shape, direction.dtype), *halves),
        [VMEM] * (3 + len(blocks)),
        (VMEM,) * (1 + len(halves)),
        scratch_shapes=[pltpu.VMEM((len(kinds) * rows, width), jnp.bfloat16)],
        input_output_aliases={2: 0},
        name="more",
    )(scale, half, direction, *blocks)
    return (direction, halves) if give else direction


def unit_kernel(raw_ref, half_ref):
    half_ref[...] = unit_half(raw_ref[...])


def normalized(raw):
    return call(unit_kernel, jax.ShapeDtypeStruct(raw.shape, raw.dtype), [VMEM], VMEM, name="unit")(raw)


def last_visits(scale, half, direction, raw, entries):
    kinds, blocks = flat(entries)
    rows, width = half.shape[1:]
    grad = jax.ShapeDtypeStruct((rows, width), jnp.float32)
    return call(
        functools.partial(last_kernel, kinds),
        (grad, grad),
        [VMEM] * (4 + len(blocks)),
        (HBM, HBM),
        scratch_shapes=[
            pltpu.VMEM(direction.shape, direction.dtype),
            pltpu.VMEM((max(1, len(kinds)) * rows, width), jnp.bfloat16),
            pltpu.VMEM(direction.shape, direction.dtype),
            pltpu.SemaphoreType.DMA((2, len(pieces(rows)))),
        ],
        name="last",
    )(scale, half, direction, raw, *blocks)


def tied(entries, *others):
    blocks, others = lax.optimization_barrier(([block for _, block in entries], others))
    return [(kind, block) for (kind, _), block in zip(entries, blocks)], *others


def on_device(
    picture_encoder_output, caption_encoder_output, softness_factor_exponent, logit_offset_term
):
    img, txt = picture_encoder_output, caption_encoder_output
    row_extent = min(8, lax.axis_size("row") // 2)
    column_extent = min(4, lax.axis_size("col") // 2)
    paired = row_extent % 2 == 0 and lax.axis_size("row") % 2 == 0
    swap = lambda s: s ^ 1
    held = [pltpu.with_memory_space_constraint(a, pltpu.HBM) for a in (img, txt)]
    text_cols, image_cols, text_rows, image_rows, swapped, last = [], [], [], [], [], []
    for k in range(1, column_extent):
        text_cols.append(((0, True), along(txt, "col", lambda s: s + k)))
    img_half, txt_half = norm(*held)
    for k in range(1, column_extent):
        image_cols.append(((1, False), along(img_half, "col", lambda s: s - k)))
    scale, raw, half, near, direction = own_visit(
        softness_factor_exponent, logit_offset_term, *held, img_half, txt_half
    )
    if not paired:
        for k in range(1, row_extent):
            text_rows.append(((0, True), along(txt, "row", lambda s: s + k)))
            image_rows.append(((1, False), along(img_half, "row", lambda s: s - k)))
        last = text_cols + image_cols + text_rows + image_rows
        return last_visits(scale, half, direction, raw, last)

    reach = row_extent - 1
    far = along(pick(*held), "row", lambda s: s + reach if s % 2 else s - reach)
    for d in range(2, row_extent, 2):
        text_rows.append(((0, True), along(txt, "row", lambda s: s + d)))
        image_rows.append(((1, False), along(img_half, "row", lambda s: s - d)))
    if text_cols:
        direction = more_visits(scale, half, direction, text_cols)
    if text_rows:
        direction, halves = more_visits(scale, half, direction, text_rows, give=True)
        per = len(halves) // len(text_rows)
        for n in range(len(text_rows)):
            block = halves[n * per : (n + 1) * per]
            swapped.append(((0, False), [along(cut, "row", swap) for cut in block]))
        direction = more_visits(scale, half, direction, swapped)
    far, direction = lax.optimization_barrier((far, direction))
    middle = image_rows + image_cols + [((2, False), normalized(far))]
    middle, near, direction = tied(middle, near, direction)
    last = [(kind, along(block, "row", swap)) for kind, block in middle[: len(image_rows)]]
    last.append(((3, False), along(near, "row", swap)))
    direction = more_visits(scale, half, direction, middle)
    return last_visits(scale, half, direction, raw, last)


def solution(mesh):
    return jax.shard_map(
        on_device,
        mesh=mesh,
        in_specs=(P(("row", "col"), None), P(("row", "col"), None), P(), P()),
        out_specs=(P(("row", "col"), None), P(("row", "col"), None)),
        check_vma=False,
    )
```

```python
import functools

import jax
import jax.numpy as jnp
from jax import lax
from jax.experimental import pallas as pl
from jax.experimental.pallas import tpu as pltpu
from jax.sharding import PartitionSpec as P

eps_norm = 1e-06
VMEM = pl.BlockSpec(memory_space=pltpu.VMEM)
SMEM = pl.BlockSpec(memory_space=pltpu.SMEM)
HBM = pl.BlockSpec(memory_space=pltpu.HBM)
LIMIT = 24 * 2**20
PIECES = 4
CUTS = 2


def along(value, axis, target):
    count = lax.axis_size(axis)
    pairs = [(source, target(source) % count) for source in range(count)]
    return lax.ppermute(value, axis, pairs)


def inverse_norm(values):
    return lax.rsqrt(jnp.sum(values * values, axis=-1, keepdims=True) + eps_norm)


def unit_half(raw):
    values = raw.astype(jnp.float32)
    return (values * inverse_norm(values)).astype(jnp.bfloat16)


def weigh(own, other, scale_ref):
    scores = lax.dot_general(
        own, other, (((1,), (1,)), ((), ())), preferred_element_type=jnp.float32
    )
    return jax.nn.sigmoid(scale_ref[0:1, 0:1] * scores + scale_ref[1:2, 0:1])


def visit(own, other, scale_ref):
    weights = scale_ref[0:1, 0:1] * weigh(own, other, scale_ref)
    return jnp.dot(weights.astype(jnp.bfloat16), other, preferred_element_type=jnp.float32)


def odd_row():
    return lax.axis_index("row") & 1


def unit_back(raw, direction):
    values = raw.astype(jnp.float32)
    inverse = inverse_norm(values)
    unit = values * inverse
    share = jnp.sum(unit * direction, axis=-1, keepdims=True)
    return inverse * (direction - unit * share)


def pieces(rows, count=PIECES):
    if rows % (16 * count):
        return [(0, rows)]
    return [(n * rows // count, rows // count) for n in range(count)]


def cuts(block):
    return [
        jax.ShapeDtypeStruct((size,) + block.shape[1:], block.dtype)
        for _, size in pieces(block.shape[0], CUTS)
    ]


def call(kernel, out_shape, in_specs, out_specs, **more):
    return pl.pallas_call(
        kernel,
        out_shape=out_shape,
        in_specs=in_specs,
        out_specs=out_specs,
        compiler_params=pltpu.CompilerParams(vmem_limit_bytes=LIMIT),
        cost_estimate=pl.CostEstimate(flops=1000, bytes_accessed=1000, transcendentals=0),
        **more,
    )


def pick_kernel(img_ref, txt_ref, out_ref, sems):
    def copy(source):
        parts = [pl.ds(start, size) for start, size in pieces(out_ref.shape[0])]
        copies = [
            pltpu.make_async_copy(source.at[at], out_ref.at[at], sems.at[n])
            for n, at in enumerate(parts)
        ]
        for one in copies:
            one.start()
        for one in copies:
            one.wait()

    odd = odd_row()

    @pl.when(odd == 1)
    def _():
        copy(txt_ref)

    @pl.when(odd != 1)
    def _():
        copy(img_ref)


def pick(img, txt):
    return call(
        pick_kernel,
        jax.ShapeDtypeStruct(img.shape, img.dtype),
        [HBM, HBM],
        VMEM,
        scratch_shapes=[pltpu.SemaphoreType.DMA((len(pieces(img.shape[0])),))],
        name="pick",
    )(img, txt)


def load(sources, raw_refs, sems):
    parts = pieces(sources[0].shape[0])
    started = []
    for side, (source, raw_ref) in enumerate(zip(sources, raw_refs)):
        started.append([])
        for n, (start, size) in enumerate(parts):
            at = pl.ds(start, size)
            copy = pltpu.make_async_copy(source.at[at], raw_ref.at[at], sems.at[side, n])
            copy.start()
            started[-1].append((at, copy))
    return started


def norm_kernel(img_ref, txt_ref, img_half, txt_half, raw_ref, sems):
    halves = (img_half, txt_half)
    started = load((img_ref, txt_ref), (raw_ref.at[0], raw_ref.at[1]), sems)
    for side, copies in enumerate(started):
        for at, copy in copies:
            copy.wait()
            halves[side][at] = unit_half(raw_ref[side, at])


def norm(img, txt):
    rows, width = img.shape
    one = jax.ShapeDtypeStruct((rows, width), jnp.bfloat16)
    return call(
        norm_kernel,
        (one, one),
        [HBM, HBM],
        (VMEM, VMEM),
        scratch_shapes=[
            pltpu.VMEM((2, rows, width), jnp.bfloat16),
            pltpu.SemaphoreType.DMA((2, len(pieces(rows)))),
        ],
        name="norm",
    )(img, txt)


def own_kernel(
    exponent_ref, offset_ref, img_ref, txt_ref, img_half, txt_half,
    scale_ref, raw_ref, half_ref, near_ref, dir_ref, sems,
):
    started = load((img_ref, txt_ref), (raw_ref.at[0], raw_ref.at[1]), sems)
    scale_ref[0:1] = jnp.exp(jnp.broadcast_to(exponent_ref[...], (1, 128)))
    scale_ref[1:2] = jnp.broadcast_to(offset_ref[...], (1, 128))
    half_ref[0] = img_half[...]
    half_ref[1] = txt_half[...]
    near_ref[...] = half_ref[1 - odd_row()]
    img, txt = half_ref[0], half_ref[1]
    rows = img.shape[0]
    row = lax.broadcasted_iota(jnp.int32, (rows, rows), 0)
    column = lax.broadcasted_iota(jnp.int32, (rows, rows), 1)
    match = jnp.where(row == column, 1.0, 0.0)
    for side, (own, other) in enumerate(((img, txt), (txt, img))):
        weights = scale_ref[0:1, 0:1] * (weigh(own, other, scale_ref) - match)
        dir_ref[side] = jnp.dot(
            weights.astype(jnp.bfloat16), other, preferred_element_type=jnp.float32
        )
    for copies in started:
        for _, copy in copies:
            copy.wait()


def own_visit(exponent, offset, img, txt, img_half, txt_half):
    rows, width = img.shape
    both = jax.ShapeDtypeStruct((2, rows, width), jnp.bfloat16)
    return call(
        own_kernel,
        (
            jax.ShapeDtypeStruct((8, 128), jnp.float32),
            both,
            both,
            jax.ShapeDtypeStruct((rows, width), jnp.bfloat16),
            jax.ShapeDtypeStruct((2, rows, width), jnp.float32),
        ),
        [VMEM, VMEM, HBM, HBM, VMEM, VMEM],
        (VMEM,) * 5,
        scratch_shapes=[pltpu.SemaphoreType.DMA((2, len(pieces(rows))))],
        name="own",
    )(exponent.reshape(1, 1), offset.reshape(1, 1), img, txt, img_half, txt_half)


def parts_of(kinds, refs, rows):
    refs, blocks = list(refs), []
    for _ in kinds:
        block = [refs.pop(0)]
        while sum(part.shape[0] for part in block) < rows:
            block.append(refs.pop(0))
        blocks.append(block)
    return blocks


def flat(entries):
    kinds = tuple(kind for kind, _ in entries)
    return kinds, jax.tree.leaves([block for _, block in entries])


def visit_all(kinds, blocks, scale_ref, half_ref, dir_ref, acc_ref, others_ref, sides=(0, 1)):
    rows = half_ref.shape[1]
    blocks = parts_of(kinds, blocks, rows)
    held = [others_ref.at[pl.ds(n * rows, rows)] for n in range(len(kinds))]
    order = sorted(range(len(kinds)), key=lambda n: kinds[n][0])
    for place, n in enumerate(order):
        start = 0
        for part in blocks[n]:
            size = part.shape[0]
            block = part[...]
            held[place][pl.ds(start, size)] = unit_half(block) if kinds[n][1] else block
            start += size
    first = 0
    for side in sides:
        count = sum(kind[0] == side for kind in kinds)
        if count:
            others = others_ref[pl.ds(first * rows, count * rows)]
            acc_ref[side] = dir_ref[side] + visit(half_ref[side], others, scale_ref)
        else:
            acc_ref[side] = dir_ref[side]
        first += count
    for place in range(first, len(kinds)):
        at = odd_row() if kinds[order[place]][0] == 2 else 1 - odd_row()
        acc_ref[at] += visit(half_ref[at], held[place][...], scale_ref)


def more_kernel(kinds, given, scale_ref, half_ref, dir_ref, *rest):
    blocks, rest = rest[: len(rest) - 2 - given], rest[len(rest) - 2 - given :]
    out_ref, halves, others_ref = rest[0], rest[1:-1], rest[-1]
    visit_all(kinds, blocks, scale_ref, half_ref, dir_ref, out_ref, others_ref)
    start = 0
    for cut in halves:
        cut[...] = others_ref[pl.ds(start, cut.shape[0])]
        start += cut.shape[0]


def finish(raw_ref, acc_ref, grad_ref, held_ref, sems):
    copies = []
    for n, (start, size) in enumerate(pieces(held_ref.shape[0])):
        at = pl.ds(start, size)
        held_ref[at] = unit_back(raw_ref[at], acc_ref[at])
        copies.append(pltpu.make_async_copy(held_ref.at[at], grad_ref.at[at], sems.at[n]))
        copies[-1].start()
    return copies


def last_kernel(kinds, scale_ref, half_ref, dir_ref, raw_ref, *rest):
    blocks, (img_grad, txt_grad, acc_ref, others_ref, held_ref, sems) = rest[:-6], rest[-6:]
    texts = [n for n, (side, _) in enumerate(kinds) if side == 1]
    late = [(kinds[n], blocks[n]) for n in texts]
    early = [(kinds[n], blocks[n]) for n in range(len(kinds)) if n not in texts]
    copies, source = [], dir_ref
    for side, entries, grad_ref in ((0, early, img_grad), (1, late, txt_grad)):
        sides = (0, 1) if side == 0 else (1,)
        visit_all(*flat(entries), scale_ref, half_ref, source, acc_ref, others_ref, sides)
        copies += finish(
            raw_ref.at[side], acc_ref.at[side], grad_ref, held_ref.at[side], sems.at[side]
        )
        source = acc_ref
    for copy in copies:
        copy.wait()


def more_visits(scale, half, direction, entries, give=False):
    kinds, blocks = flat(entries)
    rows, width = half.shape[1:]
    one = jax.ShapeDtypeStruct((rows, width), jnp.bfloat16)
    halves = cuts(one) * len(kinds) if give else []
    direction, *halves = call(
        functools.partial(more_kernel, kinds, len(halves)),
        (jax.ShapeDtypeStruct(direction.shape, direction.dtype), *halves),
        [VMEM] * (3 + len(blocks)),
        (VMEM,) * (1 + len(halves)),
        scratch_shapes=[pltpu.VMEM((len(kinds) * rows, width), jnp.bfloat16)],
        input_output_aliases={2: 0},
        name="more",
    )(scale, half, direction, *blocks)
    return (direction, halves) if give else direction


def unit_kernel(raw_ref, half_ref):
    half_ref[...] = unit_half(raw_ref[...])


def normalized(raw):
    return call(unit_kernel, jax.ShapeDtypeStruct(raw.shape, raw.dtype), [VMEM], VMEM, name="unit")(raw)


def last_visits(scale, half, direction, raw, entries):
    kinds, blocks = flat(entries)
    rows, width = half.shape[1:]
    grad = jax.ShapeDtypeStruct((rows, width), jnp.float32)
    return call(
        functools.partial(last_kernel, kinds),
        (grad, grad),
        [VMEM] * (4 + len(blocks)),
        (HBM, HBM),
        scratch_shapes=[
            pltpu.VMEM(direction.shape, direction.dtype),
            pltpu.VMEM((max(1, len(kinds)) * rows, width), jnp.bfloat16),
            pltpu.VMEM(direction.shape, direction.dtype),
            pltpu.SemaphoreType.DMA((2, len(pieces(rows)))),
        ],
        name="last",
    )(scale, half, direction, raw, *blocks)


def tied(entries, *others):
    blocks, others = lax.optimization_barrier(([block for _, block in entries], others))
    return [(kind, block) for (kind, _), block in zip(entries, blocks)], *others


def on_device(
    picture_encoder_output, caption_encoder_output, softness_factor_exponent, logit_offset_term
):
    img, txt = picture_encoder_output, caption_encoder_output
    row_extent = min(8, lax.axis_size("row") // 2)
    column_extent = min(4, lax.axis_size("col") // 2)
    paired = row_extent % 2 == 0 and lax.axis_size("row") % 2 == 0
    swap = lambda s: s ^ 1
    held = [pltpu.with_memory_space_constraint(a, pltpu.HBM) for a in (img, txt)]
    text_cols, image_cols, text_rows, image_rows, swapped, last = [], [], [], [], [], []
    for k in range(1, column_extent):
        text_cols.append(((0, True), along(txt, "col", lambda s: s + k)))
    img_half, txt_half = norm(*held)
    for k in range(1, column_extent):
        image_cols.append(((1, False), along(img_half, "col", lambda s: s - k)))
    scale, raw, half, near, direction = own_visit(
        softness_factor_exponent, logit_offset_term, *held, img_half, txt_half
    )
    if not paired:
        for k in range(1, row_extent):
            text_rows.append(((0, True), along(txt, "row", lambda s: s + k)))
            image_rows.append(((1, False), along(img_half, "row", lambda s: s - k)))
        last = text_cols + image_cols + text_rows + image_rows
        return last_visits(scale, half, direction, raw, last)

    reach = row_extent - 1
    far = along(pick(*held), "row", lambda s: s + reach if s % 2 else s - reach)
    for d in range(2, row_extent, 2):
        text_rows.append(((0, True), along(txt, "row", lambda s: s + d)))
        image_rows.append(((1, False), along(img_half, "row", lambda s: s - d)))
    if text_rows:
        direction, halves = more_visits(scale, half, direction, text_rows, give=True)
        per = len(halves) // len(text_rows)
        for n in range(len(text_rows)):
            block = halves[n * per : (n + 1) * per]
            swapped.append(((0, False), [along(cut, "row", swap) for cut in block]))
    if text_cols + swapped:
        direction = more_visits(scale, half, direction, text_cols + swapped)
    far, direction = lax.optimization_barrier((far, direction))
    middle = image_rows + image_cols + [((2, False), normalized(far))]
    middle, near, direction = tied(middle, near, direction)
    last = [(kind, along(block, "row", swap)) for kind, block in middle[: len(image_rows)]]
    last.append(((3, False), along(near, "row", swap)))
    direction = more_visits(scale, half, direction, middle)
    return last_visits(scale, half, direction, raw, last)


def solution(mesh):
    return jax.shard_map(
        on_device,
        mesh=mesh,
        in_specs=(P(("row", "col"), None), P(("row", "col"), None), P(), P()),
        out_specs=(P(("row", "col"), None), P(("row", "col"), None)),
        check_vma=False,
    )
```

```python
import functools

import jax
import jax.numpy as jnp
from jax import lax
from jax.experimental import pallas as pl
from jax.experimental.pallas import tpu as pltpu
from jax.sharding import PartitionSpec as P

eps_norm = 1e-06
VMEM = pl.BlockSpec(memory_space=pltpu.VMEM)
SMEM = pl.BlockSpec(memory_space=pltpu.SMEM)
HBM = pl.BlockSpec(memory_space=pltpu.HBM)
LIMIT = 24 * 2**20
PIECES = 4
CUTS = 1


def along(value, axis, target):
    count = lax.axis_size(axis)
    pairs = [(source, target(source) % count) for source in range(count)]
    return lax.ppermute(value, axis, pairs)


def inverse_norm(values):
    return lax.rsqrt(jnp.sum(values * values, axis=-1, keepdims=True) + eps_norm)


def unit_half(raw):
    values = raw.astype(jnp.float32)
    return (values * inverse_norm(values)).astype(jnp.bfloat16)


def weigh(own, other, scale_ref):
    scores = lax.dot_general(
        own, other, (((1,), (1,)), ((), ())), preferred_element_type=jnp.float32
    )
    return jax.nn.sigmoid(scale_ref[0:1, 0:1] * scores + scale_ref[1:2, 0:1])


def visit(own, other, scale_ref):
    weights = scale_ref[0:1, 0:1] * weigh(own, other, scale_ref)
    return jnp.dot(weights.astype(jnp.bfloat16), other, preferred_element_type=jnp.float32)


def odd_row():
    return lax.axis_index("row") & 1


def unit_back(raw, direction):
    values = raw.astype(jnp.float32)
    inverse = inverse_norm(values)
    unit = values * inverse
    share = jnp.sum(unit * direction, axis=-1, keepdims=True)
    return inverse * (direction - unit * share)


def pieces(rows, count=PIECES):
    if rows % (16 * count):
        return [(0, rows)]
    return [(n * rows // count, rows // count) for n in range(count)]


def cuts(block):
    return [
        jax.ShapeDtypeStruct((size,) + block.shape[1:], block.dtype)
        for _, size in pieces(block.shape[0], CUTS)
    ]


def call(kernel, out_shape, in_specs, out_specs, work=1000, **more):
    return pl.pallas_call(
        kernel,
        out_shape=out_shape,
        in_specs=in_specs,
        out_specs=out_specs,
        compiler_params=pltpu.CompilerParams(vmem_limit_bytes=LIMIT),
        cost_estimate=pl.CostEstimate(flops=work, bytes_accessed=work, transcendentals=0),
        **more,
    )


def pick_kernel(img_ref, txt_ref, out_ref, sems):
    def copy(source):
        parts = [pl.ds(start, size) for start, size in pieces(out_ref.shape[0])]
        copies = [
            pltpu.make_async_copy(source.at[at], out_ref.at[at], sems.at[n])
            for n, at in enumerate(parts)
        ]
        for one in copies:
            one.start()
        for one in copies:
            one.wait()

    odd = odd_row()

    @pl.when(odd == 1)
    def _():
        copy(txt_ref)

    @pl.when(odd != 1)
    def _():
        copy(img_ref)


def pick(img, txt):
    return call(
        pick_kernel,
        jax.ShapeDtypeStruct(img.shape, img.dtype),
        [HBM, HBM],
        VMEM,
        scratch_shapes=[pltpu.SemaphoreType.DMA((len(pieces(img.shape[0])),))],
        name="pick",
    )(img, txt)


def load(sources, raw_refs, sems):
    parts = pieces(sources[0].shape[0])
    started = []
    for side, (source, raw_ref) in enumerate(zip(sources, raw_refs)):
        started.append([])
        for n, (start, size) in enumerate(parts):
            at = pl.ds(start, size)
            copy = pltpu.make_async_copy(source.at[at], raw_ref.at[at], sems.at[side, n])
            copy.start()
            started[-1].append((at, copy))
    return started


def norm_kernel(img_ref, txt_ref, img_half, txt_half, raw_ref, sems):
    halves = (img_half, txt_half)
    started = load((img_ref, txt_ref), (raw_ref.at[0], raw_ref.at[1]), sems)
    for side, copies in enumerate(started):
        for at, copy in copies:
            copy.wait()
            halves[side][at] = unit_half(raw_ref[side, at])


def norm(img, txt):
    rows, width = img.shape
    one = jax.ShapeDtypeStruct((rows, width), jnp.bfloat16)
    return call(
        norm_kernel,
        (one, one),
        [HBM, HBM],
        (VMEM, VMEM),
        scratch_shapes=[
            pltpu.VMEM((2, rows, width), jnp.bfloat16),
            pltpu.SemaphoreType.DMA((2, len(pieces(rows)))),
        ],
        name="norm",
    )(img, txt)


def own_kernel(
    exponent_ref, offset_ref, img_ref, txt_ref, img_half, txt_half,
    scale_ref, raw_ref, half_ref, near_ref, dir_ref, sems,
):
    started = load((img_ref, txt_ref), (raw_ref.at[0], raw_ref.at[1]), sems)
    scale_ref[0:1] = jnp.exp(jnp.broadcast_to(exponent_ref[...], (1, 128)))
    scale_ref[1:2] = jnp.broadcast_to(offset_ref[...], (1, 128))
    half_ref[0] = img_half[...]
    half_ref[1] = txt_half[...]
    near_ref[...] = half_ref[1 - odd_row()]
    img, txt = half_ref[0], half_ref[1]
    rows = img.shape[0]
    row = lax.broadcasted_iota(jnp.int32, (rows, rows), 0)
    column = lax.broadcasted_iota(jnp.int32, (rows, rows), 1)
    match = jnp.where(row == column, 1.0, 0.0)
    for side, (own, other) in enumerate(((img, txt), (txt, img))):
        weights = scale_ref[0:1, 0:1] * (weigh(own, other, scale_ref) - match)
        dir_ref[side] = jnp.dot(
            weights.astype(jnp.bfloat16), other, preferred_element_type=jnp.float32
        )
    for copies in started:
        for _, copy in copies:
            copy.wait()


def own_visit(exponent, offset, img, txt, img_half, txt_half):
    rows, width = img.shape
    both = jax.ShapeDtypeStruct((2, rows, width), jnp.bfloat16)
    return call(
        own_kernel,
        (
            jax.ShapeDtypeStruct((8, 128), jnp.float32),
            both,
            both,
            jax.ShapeDtypeStruct((rows, width), jnp.bfloat16),
            jax.ShapeDtypeStruct((2, rows, width), jnp.float32),
        ),
        [VMEM, VMEM, HBM, HBM, VMEM, VMEM],
        (VMEM,) * 5,
        scratch_shapes=[pltpu.SemaphoreType.DMA((2, len(pieces(rows))))],
        name="own",
    )(exponent.reshape(1, 1), offset.reshape(1, 1), img, txt, img_half, txt_half)


def parts_of(kinds, refs, rows):
    refs, blocks = list(refs), []
    for _ in kinds:
        block = [refs.pop(0)]
        while sum(part.shape[0] for part in block) < rows:
            block.append(refs.pop(0))
        blocks.append(block)
    return blocks


def flat(entries):
    kinds = tuple(kind for kind, _ in entries)
    return kinds, jax.tree.leaves([block for _, block in entries])


def visit_all(kinds, blocks, scale_ref, half_ref, dir_ref, acc_ref, others_ref, sides=(0, 1)):
    rows = half_ref.shape[1]
    blocks = parts_of(kinds, blocks, rows)
    pairs = sum(side == 2 for side, _ in kinds)
    counts = [sum(kind[0] == side for kind in kinds) + pairs for side in (0, 1)]
    placed = [0, 0, 0, 0]
    for (side, raw), block in zip(kinds, blocks):
        if side < 2:
            slot = side * counts[0] + placed[side]
        else:
            to = odd_row() if side == 2 else 1 - odd_row()
            ends = [counts[0] - pairs + placed[side], sum(counts) - pairs + placed[side]]
            slot = ends[0] + to * (ends[1] - ends[0])
        placed[side] += 1
        start = slot * rows
        for part in block:
            size = part.shape[0]
            at = start if isinstance(start, int) else pl.multiple_of(start, 16)
            others_ref[pl.ds(at, size)] = unit_half(part[...]) if raw else part[...]
            start += size
    for side in sides:
        if counts[side]:
            others = others_ref[pl.ds(side * counts[0] * rows, counts[side] * rows)]
            acc_ref[side] = dir_ref[side] + visit(half_ref[side], others, scale_ref)
        else:
            acc_ref[side] = dir_ref[side]


def more_kernel(kinds, given, scale_ref, half_ref, dir_ref, *rest):
    blocks, rest = rest[: len(rest) - 2 - given], rest[len(rest) - 2 - given :]
    out_ref, halves, others_ref = rest[0], rest[1:-1], rest[-1]
    visit_all(kinds, blocks, scale_ref, half_ref, dir_ref, out_ref, others_ref)
    start = 0
    for cut in halves:
        cut[...] = others_ref[pl.ds(start, cut.shape[0])]
        start += cut.shape[0]


def finish(raw_ref, acc_ref, grad_ref, held_ref, sems):
    copies = []
    for n, (start, size) in enumerate(pieces(held_ref.shape[0])):
        at = pl.ds(start, size)
        held_ref[at] = unit_back(raw_ref[at], acc_ref[at])
        copies.append(pltpu.make_async_copy(held_ref.at[at], grad_ref.at[at], sems.at[n]))
        copies[-1].start()
    return copies


def last_kernel(kinds, scale_ref, half_ref, dir_ref, raw_ref, *rest):
    blocks, (img_grad, txt_grad, acc_ref, others_ref, held_ref, sems) = rest[:-6], rest[-6:]
    texts = any(side == 0 for side, _ in kinds)
    if texts:
        visit_all(kinds, blocks, scale_ref, half_ref, dir_ref, acc_ref, others_ref)
    source = acc_ref if texts else dir_ref
    copies = finish(raw_ref.at[0], source.at[0], img_grad, held_ref.at[0], sems.at[0])
    if not texts:
        visit_all(kinds, blocks, scale_ref, half_ref, dir_ref, acc_ref, others_ref, (1,))
    copies += finish(raw_ref.at[1], acc_ref.at[1], txt_grad, held_ref.at[1], sems.at[1])
    for copy in copies:
        copy.wait()


def more_visits(scale, half, direction, entries, give=False, work=1000):
    kinds, blocks = flat(entries)
    rows, width = half.shape[1:]
    one = jax.ShapeDtypeStruct((rows, width), jnp.bfloat16)
    halves = cuts(one) * len(kinds) if give else []
    direction, *halves = call(
        functools.partial(more_kernel, kinds, len(halves)),
        (jax.ShapeDtypeStruct(direction.shape, direction.dtype), *halves),
        [VMEM] * (3 + len(blocks)),
        (VMEM,) * (1 + len(halves)),
        scratch_shapes=[pltpu.VMEM((len(kinds) * rows, width), jnp.bfloat16)],
        input_output_aliases={2: 0},
        work=work,
        name="more",
    )(scale, half, direction, *blocks)
    return (direction, halves) if give else direction


def unit_kernel(raw_ref, half_ref):
    half_ref[...] = unit_half(raw_ref[...])


def normalized(raw):
    return call(unit_kernel, jax.ShapeDtypeStruct(raw.shape, raw.dtype), [VMEM], VMEM, name="unit")(raw)


def last_visits(scale, half, direction, raw, entries):
    kinds, blocks = flat(entries)
    rows, width = half.shape[1:]
    grad = jax.ShapeDtypeStruct((rows, width), jnp.float32)
    return call(
        functools.partial(last_kernel, kinds),
        (grad, grad),
        [VMEM] * (4 + len(blocks)),
        (HBM, HBM),
        scratch_shapes=[
            pltpu.VMEM(direction.shape, direction.dtype),
            pltpu.VMEM((max(1, len(kinds)) * rows, width), jnp.bfloat16),
            pltpu.VMEM(direction.shape, direction.dtype),
            pltpu.SemaphoreType.DMA((2, len(pieces(rows)))),
        ],
        name="last",
    )(scale, half, direction, raw, *blocks)


def tied(entries, *others):
    blocks, others = lax.optimization_barrier(([block for _, block in entries], others))
    return [(kind, block) for (kind, _), block in zip(entries, blocks)], *others


def on_device(
    picture_encoder_output, caption_encoder_output, softness_factor_exponent, logit_offset_term
):
    img, txt = picture_encoder_output, caption_encoder_output
    row_extent = min(8, lax.axis_size("row") // 2)
    column_extent = min(4, lax.axis_size("col") // 2)
    paired = row_extent % 2 == 0 and lax.axis_size("row") % 2 == 0
    swap = lambda s: s ^ 1
    held = [pltpu.with_memory_space_constraint(a, pltpu.HBM) for a in (img, txt)]
    text_cols, image_cols, text_rows, image_rows, swapped, last = [], [], [], [], [], []
    for k in range(1, column_extent):
        text_cols.append(((0, True), along(txt, "col", lambda s: s + k)))
    img_half, txt_half = norm(*held)
    for k in range(1, column_extent):
        image_cols.append(((1, False), along(img_half, "col", lambda s: s - k)))
    scale, raw, half, near, direction = own_visit(
        softness_factor_exponent, logit_offset_term, *held, img_half, txt_half
    )
    if not paired:
        for k in range(1, row_extent):
            text_rows.append(((0, True), along(txt, "row", lambda s: s + k)))
            image_rows.append(((1, False), along(img_half, "row", lambda s: s - k)))
        last = text_cols + image_cols + text_rows + image_rows
        return last_visits(scale, half, direction, raw, last)

    reach = row_extent - 1
    far = along(pick(*held), "row", lambda s: s + reach if s % 2 else s - reach)
    for d in range(2, row_extent, 2):
        text_rows.append(((0, True), along(txt, "row", lambda s: s + d)))
        image_rows.append(((1, False), along(img_half, "row", lambda s: s - d)))
    if text_rows:
        direction, halves = more_visits(scale, half, direction, text_rows, give=True)
        per = len(halves) // len(text_rows)
        for n in range(len(text_rows)):
            block = halves[n * per : (n + 1) * per]
            swapped.append(((0, False), [along(cut, "row", swap) for cut in block]))
    near, direction = lax.optimization_barrier((near, direction))
    swapped.append(((3, False), along(near, "row", swap)))
    if text_cols:
        direction = more_visits(scale, half, direction, text_cols)
    far, direction = lax.optimization_barrier((far, direction))
    middle = image_rows + image_cols + [((2, False), normalized(far))]
    middle, direction = tied(middle, direction)
    last = [(kind, along(block, "row", swap)) for kind, block in middle[: len(image_rows)]]
    direction = more_visits(scale, half, direction, middle + swapped, work=4000000)
    return last_visits(scale, half, direction, raw, last)


def solution(mesh):
    return jax.shard_map(
        on_device,
        mesh=mesh,
        in_specs=(P(("row", "col"), None), P(("row", "col"), None), P(), P()),
        out_specs=(P(("row", "col"), None), P(("row", "col"), None)),
        check_vma=False,
    )
```

```python
import functools

import jax
import jax.numpy as jnp
from jax import lax
from jax.experimental import pallas as pl
from jax.experimental.pallas import tpu as pltpu
from jax.sharding import PartitionSpec as P

eps_norm = 1e-06
VMEM = pl.BlockSpec(memory_space=pltpu.VMEM)
SMEM = pl.BlockSpec(memory_space=pltpu.SMEM)
HBM = pl.BlockSpec(memory_space=pltpu.HBM)
LIMIT = 24 * 2**20
PIECES = 4
LOG2_E = 1.4426950408889634
CUTS = 1


def along(value, axis, target):
    count = lax.axis_size(axis)
    pairs = [(source, target(source) % count) for source in range(count)]
    return lax.ppermute(value, axis, pairs)


def inverse_norm(values):
    return lax.rsqrt(jnp.sum(values * values, axis=-1, keepdims=True) + eps_norm)


def unit_half(raw):
    values = raw.astype(jnp.float32)
    return (values * inverse_norm(values)).astype(jnp.bfloat16)


def weigh(own, other, scale_ref):
    scores = lax.dot_general(
        own, other, (((1,), (1,)), ((), ())), preferred_element_type=jnp.float32
    )
    return jax.nn.sigmoid(scale_ref[0:1, 0:1] * scores + scale_ref[1:2, 0:1])


def visit(own, other, scale_ref):
    scores = lax.dot_general(
        own, other, (((1,), (1,)), ((), ())), preferred_element_type=jnp.float32
    )
    power = jnp.exp2(scale_ref[2:3, 0:1] * scores + scale_ref[3:4, 0:1])
    weights = scale_ref[0:1, 0:1] * pl.reciprocal(1.0 + power, approx=False)
    return jnp.dot(weights.astype(jnp.bfloat16), other, preferred_element_type=jnp.float32)


def odd_row():
    return lax.axis_index("row") & 1


def unit_back(raw, inverse, direction):
    values = raw.astype(jnp.float32)
    share = inverse * jnp.sum(values * direction, axis=-1, keepdims=True)
    return inverse * direction - values * (inverse * inverse * share)


def pieces(rows, count=PIECES):
    if rows % (16 * count):
        return [(0, rows)]
    return [(n * rows // count, rows // count) for n in range(count)]


def cuts(block):
    return [
        jax.ShapeDtypeStruct((size,) + block.shape[1:], block.dtype)
        for _, size in pieces(block.shape[0], CUTS)
    ]


def call(kernel, out_shape, in_specs, out_specs, work=1000, **more):
    return pl.pallas_call(
        kernel,
        out_shape=out_shape,
        in_specs=in_specs,
        out_specs=out_specs,
        compiler_params=pltpu.CompilerParams(vmem_limit_bytes=LIMIT),
        cost_estimate=pl.CostEstimate(flops=work, bytes_accessed=work, transcendentals=0),
        **more,
    )


def pick_kernel(img_ref, txt_ref, out_ref, sems):
    def copy(source):
        parts = [pl.ds(start, size) for start, size in pieces(out_ref.shape[0])]
        copies = [
            pltpu.make_async_copy(source.at[at], out_ref.at[at], sems.at[n])
            for n, at in enumerate(parts)
        ]
        for one in copies:
            one.start()
        for one in copies:
            one.wait()

    odd = odd_row()

    @pl.when(odd == 1)
    def _():
        copy(txt_ref)

    @pl.when(odd != 1)
    def _():
        copy(img_ref)


def pick(img, txt):
    return call(
        pick_kernel,
        jax.ShapeDtypeStruct(img.shape, img.dtype),
        [HBM, HBM],
        VMEM,
        scratch_shapes=[pltpu.SemaphoreType.DMA((len(pieces(img.shape[0])),))],
        name="pick",
    )(img, txt)


def load(sources, raw_refs, sems):
    parts = pieces(sources[0].shape[0])
    started = []
    for side, (source, raw_ref) in enumerate(zip(sources, raw_refs)):
        started.append([])
        for n, (start, size) in enumerate(parts):
            at = pl.ds(start, size)
            copy = pltpu.make_async_copy(source.at[at], raw_ref.at[at], sems.at[side, n])
            copy.start()
            started[-1].append((at, copy))
    return started


def norm_kernel(img_ref, img_half, raw_ref, sems):
    for at, copy in load((img_ref,), (raw_ref,), sems)[0]:
        copy.wait()
        img_half[at] = unit_half(raw_ref[at])


def norm(img):
    one = jax.ShapeDtypeStruct(img.shape, jnp.bfloat16)
    return call(
        norm_kernel,
        one,
        [HBM],
        VMEM,
        scratch_shapes=[
            pltpu.VMEM(img.shape, jnp.bfloat16),
            pltpu.SemaphoreType.DMA((1, len(pieces(img.shape[0])))),
        ],
        name="norm",
    )(img)


def own_kernel(
    exponent_ref, offset_ref, img_ref, txt_ref, img_half,
    scale_ref, raw_ref, half_ref, inverse_ref, near_ref, dir_ref, sems,
):
    started = load((img_ref, txt_ref), (raw_ref.at[0], raw_ref.at[1]), sems)
    scale_ref[0:1] = jnp.exp(jnp.broadcast_to(exponent_ref[...], (1, 128)))
    scale_ref[1:2] = jnp.broadcast_to(offset_ref[...], (1, 128))
    scale_ref[2:4] = -LOG2_E * scale_ref[0:2]
    half_ref[0] = img_half[...]
    for side in (1, 0):
        for at, copy in started[side]:
            copy.wait()
            values = raw_ref[side, at].astype(jnp.float32)
            inverse = inverse_norm(values)
            inverse_ref[side, at] = jnp.broadcast_to(inverse, (values.shape[0], 128))
            if side == 1:
                half_ref[1, at] = (values * inverse).astype(jnp.bfloat16)
    near_ref[...] = half_ref[1 - odd_row()]
    img, txt = half_ref[0], half_ref[1]
    rows = img.shape[0]
    row = lax.broadcasted_iota(jnp.int32, (rows, rows), 0)
    column = lax.broadcasted_iota(jnp.int32, (rows, rows), 1)
    match = jnp.where(row == column, 1.0, 0.0)
    for side, (own, other) in enumerate(((img, txt), (txt, img))):
        weights = scale_ref[0:1, 0:1] * (weigh(own, other, scale_ref) - match)
        dir_ref[side] = jnp.dot(
            weights.astype(jnp.bfloat16), other, preferred_element_type=jnp.float32
        )


def own_visit(exponent, offset, img, txt, img_half):
    rows, width = img.shape
    both = jax.ShapeDtypeStruct((2, rows, width), jnp.bfloat16)
    return call(
        own_kernel,
        (
            jax.ShapeDtypeStruct((8, 128), jnp.float32),
            both,
            both,
            jax.ShapeDtypeStruct((2, rows, 128), jnp.float32),
            jax.ShapeDtypeStruct((rows, width), jnp.bfloat16),
            jax.ShapeDtypeStruct((2, rows, width), jnp.float32),
        ),
        [VMEM, VMEM, HBM, HBM, VMEM],
        (VMEM,) * 6,
        scratch_shapes=[pltpu.SemaphoreType.DMA((2, len(pieces(rows))))],
        name="own",
    )(exponent.reshape(1, 1), offset.reshape(1, 1), img, txt, img_half)


def parts_of(kinds, refs, rows):
    refs, blocks = list(refs), []
    for _ in kinds:
        block = [refs.pop(0)]
        while sum(part.shape[0] for part in block) < rows:
            block.append(refs.pop(0))
        blocks.append(block)
    return blocks


def flat(entries):
    kinds = tuple(kind for kind, _ in entries)
    return kinds, jax.tree.leaves([block for _, block in entries])


def visit_all(kinds, blocks, scale_ref, half_ref, dir_ref, acc_ref, others_ref, sides=(0, 1)):
    rows = half_ref.shape[1]
    blocks = parts_of(kinds, blocks, rows)
    pairs = sum(side == 2 for side, _ in kinds)
    counts = [sum(kind[0] == side for kind in kinds) + pairs for side in (0, 1)]
    placed = [0, 0, 0, 0]
    for (side, raw), block in zip(kinds, blocks):
        if side < 2:
            slot = side * counts[0] + placed[side]
        else:
            to = odd_row() if side == 2 else 1 - odd_row()
            ends = [counts[0] - pairs + placed[side], sum(counts) - pairs + placed[side]]
            slot = ends[0] + to * (ends[1] - ends[0])
        placed[side] += 1
        start = slot * rows
        for part in block:
            size = part.shape[0]
            at = start if isinstance(start, int) else pl.multiple_of(start, 16)
            others_ref[pl.ds(at, size)] = unit_half(part[...]) if raw else part[...]
            start += size
    for side in sides:
        if counts[side]:
            others = others_ref[pl.ds(side * counts[0] * rows, counts[side] * rows)]
            acc_ref[side] = dir_ref[side] + visit(half_ref[side], others, scale_ref)
        else:
            acc_ref[side] = dir_ref[side]


def more_kernel(kinds, given, scale_ref, half_ref, dir_ref, *rest):
    blocks, rest = rest[: len(rest) - 2 - given], rest[len(rest) - 2 - given :]
    out_ref, halves, others_ref = rest[0], rest[1:-1], rest[-1]
    visit_all(kinds, blocks, scale_ref, half_ref, dir_ref, out_ref, others_ref)
    start = 0
    for cut in halves:
        cut[...] = others_ref[pl.ds(start, cut.shape[0])]
        start += cut.shape[0]


def finish(raw_ref, inverse_ref, acc_ref, grad_ref, held_ref, sems):
    copies = []
    for n, (start, size) in enumerate(pieces(held_ref.shape[0])):
        at = pl.ds(start, size)
        held_ref[at] = unit_back(raw_ref[at], inverse_ref[at][:, 0:1], acc_ref[at])
        copies.append(pltpu.make_async_copy(held_ref.at[at], grad_ref.at[at], sems.at[n]))
        copies[-1].start()
    return copies


def last_kernel(kinds, scale_ref, half_ref, dir_ref, raw_ref, inverse_ref, *rest):
    blocks, (img_grad, txt_grad, acc_ref, others_ref, held_ref, sems) = rest[:-6], rest[-6:]
    texts = any(side == 0 for side, _ in kinds)
    if texts:
        visit_all(kinds, blocks, scale_ref, half_ref, dir_ref, acc_ref, others_ref)
    source = acc_ref if texts else dir_ref
    copies = finish(
        raw_ref.at[0], inverse_ref.at[0], source.at[0], img_grad, held_ref.at[0], sems.at[0]
    )
    if not texts:
        visit_all(kinds, blocks, scale_ref, half_ref, dir_ref, acc_ref, others_ref, (1,))
    copies += finish(
        raw_ref.at[1], inverse_ref.at[1], acc_ref.at[1], txt_grad, held_ref.at[1], sems.at[1]
    )
    for copy in copies:
        copy.wait()


def more_visits(scale, half, direction, entries, give=False, work=1000):
    kinds, blocks = flat(entries)
    rows, width = half.shape[1:]
    one = jax.ShapeDtypeStruct((rows, width), jnp.bfloat16)
    halves = cuts(one) * len(kinds) if give else []
    direction, *halves = call(
        functools.partial(more_kernel, kinds, len(halves)),
        (jax.ShapeDtypeStruct(direction.shape, direction.dtype), *halves),
        [VMEM] * (3 + len(blocks)),
        (VMEM,) * (1 + len(halves)),
        scratch_shapes=[pltpu.VMEM((len(kinds) * rows, width), jnp.bfloat16)],
        input_output_aliases={2: 0},
        work=work,
        name="more",
    )(scale, half, direction, *blocks)
    return (direction, halves) if give else direction


def unit_kernel(raw_ref, half_ref):
    half_ref[...] = unit_half(raw_ref[...])


def normalized(raw):
    return call(unit_kernel, jax.ShapeDtypeStruct(raw.shape, raw.dtype), [VMEM], VMEM, name="unit")(raw)


def last_visits(scale, half, direction, raw, inverse, entries):
    kinds, blocks = flat(entries)
    rows, width = half.shape[1:]
    grad = jax.ShapeDtypeStruct((rows, width), jnp.float32)
    return call(
        functools.partial(last_kernel, kinds),
        (grad, grad),
        [VMEM] * (5 + len(blocks)),
        (HBM, HBM),
        scratch_shapes=[
            pltpu.VMEM(direction.shape, direction.dtype),
            pltpu.VMEM((max(1, len(kinds)) * rows, width), jnp.bfloat16),
            pltpu.VMEM(direction.shape, direction.dtype),
            pltpu.SemaphoreType.DMA((2, len(pieces(rows)))),
        ],
        name="last",
    )(scale, half, direction, raw, inverse, *blocks)


def tied(entries, *others):
    blocks, others = lax.optimization_barrier(([block for _, block in entries], others))
    return [(kind, block) for (kind, _), block in zip(entries, blocks)], *others


def on_device(
    picture_encoder_output, caption_encoder_output, softness_factor_exponent, logit_offset_term
):
    img, txt = picture_encoder_output, caption_encoder_output
    row_extent = min(8, lax.axis_size("row") // 2)
    column_extent = min(4, lax.axis_size("col") // 2)
    paired = row_extent % 2 == 0 and lax.axis_size("row") % 2 == 0
    swap = lambda s: s ^ 1
    held = [pltpu.with_memory_space_constraint(a, pltpu.HBM) for a in (img, txt)]
    text_cols, image_cols, text_rows, image_rows, swapped, last = [], [], [], [], [], []
    for k in range(1, column_extent):
        text_cols.append(((0, True), along(txt, "col", lambda s: s + k)))
    img_half = norm(held[0])
    for k in range(1, column_extent):
        image_cols.append(((1, False), along(img_half, "col", lambda s: s - k)))
    scale, raw, half, inverse, near, direction = own_visit(
        softness_factor_exponent, logit_offset_term, *held, img_half
    )
    if not paired:
        for k in range(1, row_extent):
            text_rows.append(((0, True), along(txt, "row", lambda s: s + k)))
            image_rows.append(((1, False), along(img_half, "row", lambda s: s - k)))
        last = text_cols + image_cols + text_rows + image_rows
        return last_visits(scale, half, direction, raw, inverse, last)

    reach = row_extent - 1
    far = along(pick(*held), "row", lambda s: s + reach if s % 2 else s - reach)
    for d in range(2, row_extent, 2):
        text_rows.append(((0, True), along(txt, "row", lambda s: s + d)))
        image_rows.append(((1, False), along(img_half, "row", lambda s: s - d)))
    if text_rows:
        direction, halves = more_visits(scale, half, direction, text_rows, give=True)
        per = len(halves) // len(text_rows)
        for n in range(len(text_rows)):
            block = halves[n * per : (n + 1) * per]
            swapped.append(((0, False), [along(cut, "row", swap) for cut in block]))
    near, direction = lax.optimization_barrier((near, direction))
    swapped.append(((3, False), along(near, "row", swap)))
    if text_cols:
        direction = more_visits(scale, half, direction, text_cols)
    far, direction = lax.optimization_barrier((far, direction))
    middle = image_rows + image_cols + [((2, False), normalized(far))]
    middle, direction = tied(middle, direction)
    last = [(kind, along(block, "row", swap)) for kind, block in middle[: len(image_rows)]]
    direction = more_visits(scale, half, direction, middle + swapped, work=4000000)
    return last_visits(scale, half, direction, raw, inverse, last)


def solution(mesh):
    return jax.shard_map(
        on_device,
        mesh=mesh,
        in_specs=(P(("row", "col"), None), P(("row", "col"), None), P(), P()),
        out_specs=(P(("row", "col"), None), P(("row", "col"), None)),
        check_vma=False,
    )
```

```python
import functools

import jax
import jax.numpy as jnp
from jax import lax
from jax.experimental import pallas as pl
from jax.experimental.pallas import tpu as pltpu
from jax.sharding import PartitionSpec as P

eps_norm = 1e-06
VMEM = pl.BlockSpec(memory_space=pltpu.VMEM)
SMEM = pl.BlockSpec(memory_space=pltpu.SMEM)
HBM = pl.BlockSpec(memory_space=pltpu.HBM)
LIMIT = 24 * 2**20
PIECES = 4
LOG2_E = 1.4426950408889634
CUTS = 1


def along(value, axis, target):
    count = lax.axis_size(axis)
    pairs = [(source, target(source) % count) for source in range(count)]
    return lax.ppermute(value, axis, pairs)


def inverse_norm(values):
    return lax.rsqrt(jnp.sum(values * values, axis=-1, keepdims=True) + eps_norm)


def unit_half(raw):
    values = raw.astype(jnp.float32)
    return (values * inverse_norm(values)).astype(jnp.bfloat16)


def weigh(own, other, scale_ref):
    scores = lax.dot_general(
        own, other, (((1,), (1,)), ((), ())), preferred_element_type=jnp.float32
    )
    return jax.nn.sigmoid(scale_ref[0:1, 0:1] * scores + scale_ref[1:2, 0:1])


def visit(own, other, scale_ref):
    scores = lax.dot_general(
        own, other, (((1,), (1,)), ((), ())), preferred_element_type=jnp.float32
    )
    power = jnp.exp2(scale_ref[2:3, 0:1] * scores + scale_ref[3:4, 0:1])
    weights = scale_ref[0:1, 0:1] * pl.reciprocal(1.0 + power, approx=False)
    return jnp.dot(weights.astype(jnp.bfloat16), other, preferred_element_type=jnp.float32)


def odd_row():
    return lax.axis_index("row") & 1


def unit_back(raw, inverse, direction):
    values = raw.astype(jnp.float32)
    share = inverse * jnp.sum(values * direction, axis=-1, keepdims=True)
    return inverse * direction - values * (inverse * inverse * share)


def pieces(rows, count=PIECES):
    if rows % (16 * count):
        return [(0, rows)]
    return [(n * rows // count, rows // count) for n in range(count)]


def cuts(block):
    return [
        jax.ShapeDtypeStruct((size,) + block.shape[1:], block.dtype)
        for _, size in pieces(block.shape[0], CUTS)
    ]


def call(kernel, out_shape, in_specs, out_specs, work=1000, **more):
    return pl.pallas_call(
        kernel,
        out_shape=out_shape,
        in_specs=in_specs,
        out_specs=out_specs,
        compiler_params=pltpu.CompilerParams(vmem_limit_bytes=LIMIT),
        cost_estimate=pl.CostEstimate(flops=work, bytes_accessed=work, transcendentals=0),
        **more,
    )


def pick_kernel(img_ref, txt_ref, out_ref, sems):
    def copy(source):
        parts = [pl.ds(start, size) for start, size in pieces(out_ref.shape[0])]
        copies = [
            pltpu.make_async_copy(source.at[at], out_ref.at[at], sems.at[n])
            for n, at in enumerate(parts)
        ]
        for one in copies:
            one.start()
        for one in copies:
            one.wait()

    odd = odd_row()

    @pl.when(odd == 1)
    def _():
        copy(txt_ref)

    @pl.when(odd != 1)
    def _():
        copy(img_ref)


def pick(img, txt):
    return call(
        pick_kernel,
        jax.ShapeDtypeStruct(img.shape, img.dtype),
        [HBM, HBM],
        VMEM,
        scratch_shapes=[pltpu.SemaphoreType.DMA((len(pieces(img.shape[0])),))],
        name="pick",
    )(img, txt)


def load(sources, raw_refs, sems):
    parts = pieces(sources[0].shape[0])
    started = []
    for side, (source, raw_ref) in enumerate(zip(sources, raw_refs)):
        started.append([])
        for n, (start, size) in enumerate(parts):
            at = pl.ds(start, size)
            copy = pltpu.make_async_copy(source.at[at], raw_ref.at[at], sems.at[side, n])
            copy.start()
            started[-1].append((at, copy))
    return started


def norm_kernel(img_ref, img_half, raw_ref, sems):
    for at, copy in load((img_ref,), (raw_ref,), sems)[0]:
        copy.wait()
        img_half[at] = unit_half(raw_ref[at])


def norm(img):
    one = jax.ShapeDtypeStruct(img.shape, jnp.bfloat16)
    return call(
        norm_kernel,
        one,
        [HBM],
        VMEM,
        scratch_shapes=[
            pltpu.VMEM(img.shape, jnp.bfloat16),
            pltpu.SemaphoreType.DMA((1, len(pieces(img.shape[0])))),
        ],
        name="norm",
    )(img)


def own_kernel(
    exponent_ref, offset_ref, img_ref, txt_ref, img_half,
    scale_ref, raw_ref, half_ref, inverse_ref, near_ref, dir_ref, sems,
):
    started = load((img_ref, txt_ref), (raw_ref.at[0], raw_ref.at[1]), sems)
    scale_ref[0:1] = jnp.exp(jnp.broadcast_to(exponent_ref[...], (1, 128)))
    scale_ref[1:2] = jnp.broadcast_to(offset_ref[...], (1, 128))
    scale_ref[2:4] = -LOG2_E * scale_ref[0:2]
    half_ref[0] = img_half[...]
    for side in (1, 0):
        for at, copy in started[side]:
            copy.wait()
            values = raw_ref[side, at].astype(jnp.float32)
            inverse = inverse_norm(values)
            inverse_ref[side, at] = jnp.broadcast_to(inverse, (values.shape[0], 128))
            if side == 1:
                half_ref[1, at] = (values * inverse).astype(jnp.bfloat16)
    near_ref[...] = half_ref[1 - odd_row()]
    img, txt = half_ref[0], half_ref[1]
    rows = img.shape[0]
    row = lax.broadcasted_iota(jnp.int32, (rows, rows), 0)
    column = lax.broadcasted_iota(jnp.int32, (rows, rows), 1)
    match = jnp.where(row == column, 1.0, 0.0)
    for side, (own, other) in enumerate(((img, txt), (txt, img))):
        weights = scale_ref[0:1, 0:1] * (weigh(own, other, scale_ref) - match)
        dir_ref[side] = jnp.dot(
            weights.astype(jnp.bfloat16), other, preferred_element_type=jnp.float32
        )


def own_visit(exponent, offset, img, txt, img_half):
    rows, width = img.shape
    both = jax.ShapeDtypeStruct((2, rows, width), jnp.bfloat16)
    return call(
        own_kernel,
        (
            jax.ShapeDtypeStruct((8, 128), jnp.float32),
            both,
            both,
            jax.ShapeDtypeStruct((2, rows, 128), jnp.float32),
            jax.ShapeDtypeStruct((rows, width), jnp.bfloat16),
            jax.ShapeDtypeStruct((2, rows, width), jnp.float32),
        ),
        [VMEM, VMEM, HBM, HBM, VMEM],
        (VMEM,) * 6,
        scratch_shapes=[pltpu.SemaphoreType.DMA((2, len(pieces(rows))))],
        name="own",
    )(exponent.reshape(1, 1), offset.reshape(1, 1), img, txt, img_half)


def parts_of(kinds, refs, rows):
    refs, blocks = list(refs), []
    for _ in kinds:
        block = [refs.pop(0)]
        while sum(part.shape[0] for part in block) < rows:
            block.append(refs.pop(0))
        blocks.append(block)
    return blocks


def flat(entries):
    kinds = tuple(kind for kind, _ in entries)
    return kinds, jax.tree.leaves([block for _, block in entries])


def place_all(kinds, blocks, rows, others_ref):
    blocks = parts_of(kinds, blocks, rows)
    pairs = sum(side == 2 for side, _ in kinds)
    counts = [sum(kind[0] == side for kind in kinds) + pairs for side in (0, 1)]
    placed = [0, 0, 0, 0]
    for (side, raw), block in zip(kinds, blocks):
        if side < 2:
            slot = side * counts[0] + placed[side]
        else:
            to = odd_row() if side == 2 else 1 - odd_row()
            ends = [counts[0] - pairs + placed[side], sum(counts) - pairs + placed[side]]
            slot = ends[0] + to * (ends[1] - ends[0])
        placed[side] += 1
        start = slot * rows
        for part in block:
            size = part.shape[0]
            at = start if isinstance(start, int) else pl.multiple_of(start, 16)
            others_ref[pl.ds(at, size)] = unit_half(part[...]) if raw else part[...]
            start += size
    return counts


def visit_side(side, counts, scale_ref, half_ref, dir_ref, acc_ref, others_ref):
    rows = half_ref.shape[1]
    if counts[side]:
        others = others_ref[pl.ds(side * counts[0] * rows, counts[side] * rows)]
        acc_ref[side] = dir_ref[side] + visit(half_ref[side], others, scale_ref)
    else:
        acc_ref[side] = dir_ref[side]


def visit_all(kinds, blocks, scale_ref, half_ref, dir_ref, acc_ref, others_ref):
    counts = place_all(kinds, blocks, half_ref.shape[1], others_ref)
    for side in (0, 1):
        visit_side(side, counts, scale_ref, half_ref, dir_ref, acc_ref, others_ref)


def more_kernel(kinds, given, scale_ref, half_ref, dir_ref, *rest):
    blocks, rest = rest[: len(rest) - 2 - given], rest[len(rest) - 2 - given :]
    out_ref, halves, others_ref = rest[0], rest[1:-1], rest[-1]
    visit_all(kinds, blocks, scale_ref, half_ref, dir_ref, out_ref, others_ref)
    start = 0
    for cut in halves:
        cut[...] = others_ref[pl.ds(start, cut.shape[0])]
        start += cut.shape[0]


def finish(raw_ref, inverse_ref, acc_ref, grad_ref, held_ref, sems):
    copies = []
    for n, (start, size) in enumerate(pieces(held_ref.shape[0])):
        at = pl.ds(start, size)
        held_ref[at] = unit_back(raw_ref[at], inverse_ref[at][:, 0:1], acc_ref[at])
        copies.append(pltpu.make_async_copy(held_ref.at[at], grad_ref.at[at], sems.at[n]))
        copies[-1].start()
    return copies


def image_kernel(kinds, scale_ref, half_ref, dir_ref, raw_ref, inverse_ref, *rest):
    blocks, (out_ref, img_grad, others_ref, held_ref, sems) = rest[:-5], rest[-5:]
    counts = place_all(kinds, blocks, half_ref.shape[1], others_ref)
    visit_side(0, counts, scale_ref, half_ref, dir_ref, out_ref, others_ref)
    copies = finish(
        raw_ref.at[0], inverse_ref.at[0], out_ref.at[0], img_grad, held_ref, sems
    )
    visit_side(1, counts, scale_ref, half_ref, dir_ref, out_ref, others_ref)
    for copy in copies:
        copy.wait()


def text_kernel(kinds, scale_ref, half_ref, dir_ref, raw_ref, inverse_ref, *rest):
    blocks, (txt_grad, acc_ref, others_ref, held_ref, sems) = rest[:-5], rest[-5:]
    counts = place_all(kinds, blocks, half_ref.shape[1], others_ref)
    visit_side(1, counts, scale_ref, half_ref, dir_ref, acc_ref, others_ref)
    for copy in finish(
        raw_ref.at[1], inverse_ref.at[1], acc_ref.at[1], txt_grad, held_ref, sems
    ):
        copy.wait()


def more_visits(scale, half, direction, entries, give=False, work=1000):
    kinds, blocks = flat(entries)
    rows, width = half.shape[1:]
    one = jax.ShapeDtypeStruct((rows, width), jnp.bfloat16)
    halves = cuts(one) * len(kinds) if give else []
    direction, *halves = call(
        functools.partial(more_kernel, kinds, len(halves)),
        (jax.ShapeDtypeStruct(direction.shape, direction.dtype), *halves),
        [VMEM] * (3 + len(blocks)),
        (VMEM,) * (1 + len(halves)),
        scratch_shapes=[pltpu.VMEM((len(kinds) * rows, width), jnp.bfloat16)],
        input_output_aliases={2: 0},
        work=work,
        name="more",
    )(scale, half, direction, *blocks)
    return (direction, halves) if give else direction


def unit_kernel(raw_ref, half_ref):
    half_ref[...] = unit_half(raw_ref[...])


def normalized(raw):
    return call(unit_kernel, jax.ShapeDtypeStruct(raw.shape, raw.dtype), [VMEM], VMEM, name="unit")(raw)


def grad_visits(kernel, scale, half, direction, raw, inverse, entries, work=1000):
    kinds, blocks = flat(entries)
    rows, width = half.shape[1:]
    sums = jax.ShapeDtypeStruct(direction.shape, direction.dtype)
    grad = jax.ShapeDtypeStruct((rows, width), jnp.float32)
    scratch = [
        pltpu.VMEM((max(1, len(kinds)) * rows, width), jnp.bfloat16),
        pltpu.VMEM(grad.shape, grad.dtype),
        pltpu.SemaphoreType.DMA((len(pieces(rows)),)),
    ]
    image = kernel is image_kernel
    return call(
        functools.partial(kernel, kinds),
        (sums, grad) if image else grad,
        [VMEM] * (5 + len(blocks)),
        (VMEM, HBM) if image else HBM,
        work=work,
        scratch_shapes=scratch if image else [pltpu.VMEM(sums.shape, sums.dtype)] + scratch,
        input_output_aliases={2: 0} if image else {},
        name="image" if image else "text",
    )(scale, half, direction, raw, inverse, *blocks)


def tied(entries, *others):
    blocks, others = lax.optimization_barrier(([block for _, block in entries], others))
    return [(kind, block) for (kind, _), block in zip(entries, blocks)], *others


def on_device(
    picture_encoder_output, caption_encoder_output, softness_factor_exponent, logit_offset_term
):
    img, txt = picture_encoder_output, caption_encoder_output
    row_extent = min(8, lax.axis_size("row") // 2)
    column_extent = min(4, lax.axis_size("col") // 2)
    paired = row_extent % 2 == 0 and lax.axis_size("row") % 2 == 0
    swap = lambda s: s ^ 1
    held = [pltpu.with_memory_space_constraint(a, pltpu.HBM) for a in (img, txt)]
    text_cols, image_cols, text_rows, image_rows, swapped, last = [], [], [], [], [], []
    for k in range(1, column_extent):
        text_cols.append(((0, True), along(txt, "col", lambda s: s + k)))
    img_half = norm(held[0])
    for k in range(1, column_extent):
        image_cols.append(((1, False), along(img_half, "col", lambda s: s - k)))
    scale, raw, half, inverse, near, direction = own_visit(
        softness_factor_exponent, logit_offset_term, *held, img_half
    )
    if not paired:
        for k in range(1, row_extent):
            text_rows.append(((0, True), along(txt, "row", lambda s: s + k)))
            image_rows.append(((1, False), along(img_half, "row", lambda s: s - k)))
        entries = text_cols + image_cols + text_rows + image_rows
        direction, image_grad = grad_visits(
            image_kernel, scale, half, direction, raw, inverse, entries
        )
        return image_grad, grad_visits(text_kernel, scale, half, direction, raw, inverse, [])

    reach = row_extent - 1
    far = along(pick(*held), "row", lambda s: s + reach if s % 2 else s - reach)
    for d in range(2, row_extent, 2):
        text_rows.append(((0, True), along(txt, "row", lambda s: s + d)))
        image_rows.append(((1, False), along(img_half, "row", lambda s: s - d)))
    if text_rows:
        direction, halves = more_visits(scale, half, direction, text_rows, give=True)
        per = len(halves) // len(text_rows)
        for n in range(len(text_rows)):
            block = halves[n * per : (n + 1) * per]
            swapped.append(((0, False), [along(cut, "row", swap) for cut in block]))
    near, direction = lax.optimization_barrier((near, direction))
    swapped.append(((3, False), along(near, "row", swap)))
    if text_cols:
        direction = more_visits(scale, half, direction, text_cols)
    far, direction = lax.optimization_barrier((far, direction))
    middle = image_rows + image_cols + [((2, False), normalized(far))]
    middle, direction = tied(middle, direction)
    last = [(kind, along(block, "row", swap)) for kind, block in middle[: len(image_rows)]]
    direction, image_grad = grad_visits(
        image_kernel, scale, half, direction, raw, inverse, middle + swapped, work=4000000
    )
    return image_grad, grad_visits(text_kernel, scale, half, direction, raw, inverse, last)


def solution(mesh):
    return jax.shard_map(
        on_device,
        mesh=mesh,
        in_specs=(P(("row", "col"), None), P(("row", "col"), None), P(), P()),
        out_specs=(P(("row", "col"), None), P(("row", "col"), None)),
        check_vma=False,
    )
```

```python
import functools

import jax
import jax.numpy as jnp
from jax import lax
from jax.experimental import pallas as pl
from jax.experimental.pallas import tpu as pltpu
from jax.sharding import PartitionSpec as P

eps_norm = 1e-06
VMEM = pl.BlockSpec(memory_space=pltpu.VMEM)
SMEM = pl.BlockSpec(memory_space=pltpu.SMEM)
HBM = pl.BlockSpec(memory_space=pltpu.HBM)
LIMIT = 24 * 2**20
PIECES = 4
LOG2_E = 1.4426950408889634
CUTS = 1


def along(value, axis, target):
    count = lax.axis_size(axis)
    pairs = [(source, target(source) % count) for source in range(count)]
    return lax.ppermute(value, axis, pairs)


def inverse_norm(values):
    return lax.rsqrt(jnp.sum(values * values, axis=-1, keepdims=True) + eps_norm)


def unit_half(raw):
    values = raw.astype(jnp.float32)
    return (values * inverse_norm(values)).astype(jnp.bfloat16)


def weigh(own, other, scale_ref):
    scores = lax.dot_general(
        own, other, (((1,), (1,)), ((), ())), preferred_element_type=jnp.float32
    )
    return jax.nn.sigmoid(scale_ref[0:1, 0:1] * scores + scale_ref[1:2, 0:1])


def visit(own, other, scale_ref):
    scores = lax.dot_general(
        own, other, (((1,), (1,)), ((), ())), preferred_element_type=jnp.float32
    )
    power = jnp.exp2(scale_ref[2:3, 0:1] * scores + scale_ref[3:4, 0:1])
    weights = scale_ref[0:1, 0:1] * pl.reciprocal(1.0 + power, approx=False)
    return jnp.dot(weights.astype(jnp.bfloat16), other, preferred_element_type=jnp.float32)


def odd_row():
    return lax.axis_index("row") & 1


def unit_back(raw, inverse, direction):
    values = raw.astype(jnp.float32)
    share = inverse * jnp.sum(values * direction, axis=-1, keepdims=True)
    return inverse * direction - values * (inverse * inverse * share)


def pieces(rows, count=PIECES):
    if rows % (16 * count):
        return [(0, rows)]
    return [(n * rows // count, rows // count) for n in range(count)]


def cuts(block):
    return [
        jax.ShapeDtypeStruct((size,) + block.shape[1:], block.dtype)
        for _, size in pieces(block.shape[0], CUTS)
    ]


def call(kernel, out_shape, in_specs, out_specs, work=1000, **more):
    return pl.pallas_call(
        kernel,
        out_shape=out_shape,
        in_specs=in_specs,
        out_specs=out_specs,
        compiler_params=pltpu.CompilerParams(vmem_limit_bytes=LIMIT),
        cost_estimate=pl.CostEstimate(flops=work, bytes_accessed=work, transcendentals=0),
        **more,
    )


def pick_kernel(img_ref, txt_ref, out_ref, sems):
    def copy(source):
        parts = [pl.ds(start, size) for start, size in pieces(out_ref.shape[0])]
        copies = [
            pltpu.make_async_copy(source.at[at], out_ref.at[at], sems.at[n])
            for n, at in enumerate(parts)
        ]
        for one in copies:
            one.start()
        for one in copies:
            one.wait()

    odd = odd_row()

    @pl.when(odd == 1)
    def _():
        copy(txt_ref)

    @pl.when(odd != 1)
    def _():
        copy(img_ref)


def pick(img, txt):
    return call(
        pick_kernel,
        jax.ShapeDtypeStruct(img.shape, img.dtype),
        [HBM, HBM],
        VMEM,
        scratch_shapes=[pltpu.SemaphoreType.DMA((len(pieces(img.shape[0])),))],
        name="pick",
    )(img, txt)


def load(sources, raw_refs, sems):
    parts = pieces(sources[0].shape[0])
    started = []
    for side, (source, raw_ref) in enumerate(zip(sources, raw_refs)):
        started.append([])
        for n, (start, size) in enumerate(parts):
            at = pl.ds(start, size)
            copy = pltpu.make_async_copy(source.at[at], raw_ref.at[at], sems.at[side, n])
            copy.start()
            started[-1].append((at, copy))
    return started


def norm_kernel(img_ref, img_half, raw_ref, sems):
    for at, copy in load((img_ref,), (raw_ref,), sems)[0]:
        copy.wait()
        img_half[at] = unit_half(raw_ref[at])


def norm(img):
    one = jax.ShapeDtypeStruct(img.shape, jnp.bfloat16)
    return call(
        norm_kernel,
        one,
        [HBM],
        VMEM,
        scratch_shapes=[
            pltpu.VMEM(img.shape, jnp.bfloat16),
            pltpu.SemaphoreType.DMA((1, len(pieces(img.shape[0])))),
        ],
        name="norm",
    )(img)


def own_kernel(
    exponent_ref, offset_ref, img_ref, txt_ref, img_half,
    scale_ref, raw_ref, half_ref, inverse_ref, near_ref, dir_ref, sems,
):
    started = load((img_ref, txt_ref), (raw_ref.at[0], raw_ref.at[1]), sems)
    scale_ref[0:1] = jnp.exp(jnp.broadcast_to(exponent_ref[...], (1, 128)))
    scale_ref[1:2] = jnp.broadcast_to(offset_ref[...], (1, 128))
    scale_ref[2:4] = -LOG2_E * scale_ref[0:2]
    half_ref[0] = img_half[...]
    for side in (1, 0):
        for at, copy in started[side]:
            copy.wait()
            values = raw_ref[side, at].astype(jnp.float32)
            inverse = inverse_norm(values)
            inverse_ref[side, at] = jnp.broadcast_to(inverse, (values.shape[0], 128))
            if side == 1:
                half_ref[1, at] = (values * inverse).astype(jnp.bfloat16)
    near_ref[...] = half_ref[1 - odd_row()]
    img, txt = half_ref[0], half_ref[1]
    rows = img.shape[0]
    row = lax.broadcasted_iota(jnp.int32, (rows, rows), 0)
    column = lax.broadcasted_iota(jnp.int32, (rows, rows), 1)
    match = jnp.where(row == column, 1.0, 0.0)
    for side, (own, other) in enumerate(((img, txt), (txt, img))):
        weights = scale_ref[0:1, 0:1] * (weigh(own, other, scale_ref) - match)
        dir_ref[side] = jnp.dot(
            weights.astype(jnp.bfloat16), other, preferred_element_type=jnp.float32
        )


def own_visit(exponent, offset, img, txt, img_half):
    rows, width = img.shape
    both = jax.ShapeDtypeStruct((2, rows, width), jnp.bfloat16)
    return call(
        own_kernel,
        (
            jax.ShapeDtypeStruct((8, 128), jnp.float32),
            both,
            both,
            jax.ShapeDtypeStruct((2, rows, 128), jnp.float32),
            jax.ShapeDtypeStruct((rows, width), jnp.bfloat16),
            jax.ShapeDtypeStruct((2, rows, width), jnp.float32),
        ),
        [VMEM, VMEM, HBM, HBM, VMEM],
        (VMEM,) * 6,
        scratch_shapes=[pltpu.SemaphoreType.DMA((2, len(pieces(rows))))],
        name="own",
    )(exponent.reshape(1, 1), offset.reshape(1, 1), img, txt, img_half)


def parts_of(kinds, refs, rows):
    refs, blocks = list(refs), []
    for _ in kinds:
        block = [refs.pop(0)]
        while sum(part.shape[0] for part in block) < rows:
            block.append(refs.pop(0))
        blocks.append(block)
    return blocks


def flat(entries):
    kinds = tuple(kind for kind, _ in entries)
    return kinds, jax.tree.leaves([block for _, block in entries])


def place_all(kinds, blocks, rows, others_ref):
    blocks = parts_of(kinds, blocks, rows)
    pairs = sum(side == 2 for side, _ in kinds)
    counts = [sum(kind[0] == side for kind in kinds) + pairs for side in (0, 1)]
    placed = [0, 0, 0, 0]
    for (side, raw), block in zip(kinds, blocks):
        if side < 2:
            slot = side * counts[0] + placed[side]
        else:
            to = odd_row() if side == 2 else 1 - odd_row()
            ends = [counts[0] - pairs + placed[side], sum(counts) - pairs + placed[side]]
            slot = ends[0] + to * (ends[1] - ends[0])
        placed[side] += 1
        start = slot * rows
        for part in block:
            size = part.shape[0]
            at = start if isinstance(start, int) else pl.multiple_of(start, 16)
            others_ref[pl.ds(at, size)] = unit_half(part[...]) if raw else part[...]
            start += size
    return counts


def visit_side(side, counts, scale_ref, half_ref, dir_ref, acc_ref, others_ref):
    rows = half_ref.shape[1]
    if counts[side]:
        others = others_ref[pl.ds(side * counts[0] * rows, counts[side] * rows)]
        acc_ref[side] = dir_ref[side] + visit(half_ref[side], others, scale_ref)
    else:
        acc_ref[side] = dir_ref[side]


def visit_all(kinds, blocks, scale_ref, half_ref, dir_ref, acc_ref, others_ref):
    counts = place_all(kinds, blocks, half_ref.shape[1], others_ref)
    for side in (0, 1):
        visit_side(side, counts, scale_ref, half_ref, dir_ref, acc_ref, others_ref)


def more_kernel(kinds, given, scale_ref, half_ref, dir_ref, *rest):
    blocks, rest = rest[: len(rest) - 2 - given], rest[len(rest) - 2 - given :]
    out_ref, halves, others_ref = rest[0], rest[1:-1], rest[-1]
    visit_all(kinds, blocks, scale_ref, half_ref, dir_ref, out_ref, others_ref)
    start = 0
    for cut in halves:
        cut[...] = others_ref[pl.ds(start, cut.shape[0])]
        start += cut.shape[0]


def finish(raw_ref, inverse_ref, acc_ref, grad_ref, held_ref, sems):
    copies = []
    for n, (start, size) in enumerate(pieces(held_ref.shape[0])):
        at = pl.ds(start, size)
        held_ref[at] = unit_back(raw_ref[at], inverse_ref[at][:, 0:1], acc_ref[at])
        copies.append(pltpu.make_async_copy(held_ref.at[at], grad_ref.at[at], sems.at[n]))
        copies[-1].start()
    return copies


def image_kernel(kinds, scale_ref, half_ref, dir_ref, raw_ref, inverse_ref, *rest):
    blocks, (out_ref, img_grad, others_ref, held_ref, sems) = rest[:-5], rest[-5:]
    counts = place_all(kinds, blocks, half_ref.shape[1], others_ref)
    visit_side(0, counts, scale_ref, half_ref, dir_ref, out_ref, others_ref)
    copies = finish(
        raw_ref.at[0], inverse_ref.at[0], out_ref.at[0], img_grad, held_ref, sems
    )
    visit_side(1, counts, scale_ref, half_ref, dir_ref, out_ref, others_ref)
    for copy in copies:
        copy.wait()


def text_kernel(kinds, scale_ref, half_ref, dir_ref, raw_ref, inverse_ref, *rest):
    blocks, (txt_grad, acc_ref, others_ref, held_ref, sems) = rest[:-5], rest[-5:]
    counts = place_all(kinds, blocks, half_ref.shape[1], others_ref)
    visit_side(1, counts, scale_ref, half_ref, dir_ref, acc_ref, others_ref)
    for copy in finish(
        raw_ref.at[1], inverse_ref.at[1], acc_ref.at[1], txt_grad, held_ref, sems
    ):
        copy.wait()


def more_visits(scale, half, direction, entries, give=False, work=1000):
    kinds, blocks = flat(entries)
    rows, width = half.shape[1:]
    one = jax.ShapeDtypeStruct((rows, width), jnp.bfloat16)
    halves = cuts(one) * len(kinds) if give else []
    direction, *halves = call(
        functools.partial(more_kernel, kinds, len(halves)),
        (jax.ShapeDtypeStruct(direction.shape, direction.dtype), *halves),
        [VMEM] * (3 + len(blocks)),
        (VMEM,) * (1 + len(halves)),
        scratch_shapes=[pltpu.VMEM((len(kinds) * rows, width), jnp.bfloat16)],
        input_output_aliases={2: 0},
        work=work,
        name="more",
    )(scale, half, direction, *blocks)
    return (direction, halves) if give else direction


def unit_kernel(raw_ref, half_ref):
    half_ref[...] = unit_half(raw_ref[...])


def normalized(raw):
    return call(unit_kernel, jax.ShapeDtypeStruct(raw.shape, raw.dtype), [VMEM], VMEM, name="unit")(raw)


def grad_visits(kernel, scale, half, direction, raw, inverse, entries, work=1000):
    kinds, blocks = flat(entries)
    rows, width = half.shape[1:]
    sums = jax.ShapeDtypeStruct(direction.shape, direction.dtype)
    grad = jax.ShapeDtypeStruct((rows, width), jnp.float32)
    scratch = [
        pltpu.VMEM((max(1, len(kinds)) * rows, width), jnp.bfloat16),
        pltpu.VMEM(grad.shape, grad.dtype),
        pltpu.SemaphoreType.DMA((len(pieces(rows)),)),
    ]
    image = kernel is image_kernel
    return call(
        functools.partial(kernel, kinds),
        (sums, grad) if image else grad,
        [VMEM] * (5 + len(blocks)),
        (VMEM, HBM) if image else HBM,
        work=work,
        scratch_shapes=scratch if image else [pltpu.VMEM(sums.shape, sums.dtype)] + scratch,
        input_output_aliases={2: 0} if image else {},
        name="image" if image else "text",
    )(scale, half, direction, raw, inverse, *blocks)


def tied(entries, *others):
    blocks, others = lax.optimization_barrier(([block for _, block in entries], others))
    return [(kind, block) for (kind, _), block in zip(entries, blocks)], *others


def on_device(
    picture_encoder_output, caption_encoder_output, softness_factor_exponent, logit_offset_term
):
    img, txt = picture_encoder_output, caption_encoder_output
    row_extent = min(8, lax.axis_size("row") // 2)
    column_extent = min(4, lax.axis_size("col") // 2)
    paired = row_extent % 2 == 0 and lax.axis_size("row") % 2 == 0
    swap = lambda s: s ^ 1
    held = [pltpu.with_memory_space_constraint(a, pltpu.HBM) for a in (img, txt)]
    text_cols, image_cols, text_rows, image_rows, swapped, last = [], [], [], [], [], []
    for k in range(1, column_extent):
        text_cols.append(((0, True), along(txt, "col", lambda s: s + k)))
    img_half = norm(held[0])
    for k in range(1, column_extent):
        image_cols.append(((1, False), along(img_half, "col", lambda s: s - k)))
    scale, raw, half, inverse, near, direction = own_visit(
        softness_factor_exponent, logit_offset_term, *held, img_half
    )
    if not paired:
        for k in range(1, row_extent):
            text_rows.append(((0, True), along(txt, "row", lambda s: s + k)))
            image_rows.append(((1, False), along(img_half, "row", lambda s: s - k)))
        entries = text_cols + image_cols + text_rows + image_rows
        direction, image_grad = grad_visits(
            image_kernel, scale, half, direction, raw, inverse, entries
        )
        return image_grad, grad_visits(text_kernel, scale, half, direction, raw, inverse, [])

    reach = row_extent - 1
    far = along(pick(*held), "row", lambda s: s + reach if s % 2 else s - reach)
    for d in range(2, row_extent, 2):
        text_rows.append(((0, True), along(txt, "row", lambda s: s + d)))
        image_rows.append(((1, False), along(img_half, "row", lambda s: s - d)))
    if text_rows:
        direction, halves = more_visits(scale, half, direction, text_rows, give=True)
        per = len(halves) // len(text_rows)
        for n in range(len(text_rows)):
            block = halves[n * per : (n + 1) * per]
            swapped.append(((0, False), [along(cut, "row", swap) for cut in block]))
    near, direction = lax.optimization_barrier((near, direction))
    swapped.append(((3, False), along(near, "row", swap)))
    if text_cols:
        direction = more_visits(scale, half, direction, text_cols)
    far, direction = lax.optimization_barrier((far, direction))
    last = [(kind, along(block, "row", swap)) for kind, block in image_rows]
    middle = image_rows + image_cols + [((2, False), normalized(far))]
    direction, image_grad = grad_visits(
        image_kernel, scale, half, direction, raw, inverse, middle + swapped, work=100000000
    )
    return image_grad, grad_visits(text_kernel, scale, half, direction, raw, inverse, last)


def solution(mesh):
    return jax.shard_map(
        on_device,
        mesh=mesh,
        in_specs=(P(("row", "col"), None), P(("row", "col"), None), P(), P()),
        out_specs=(P(("row", "col"), None), P(("row", "col"), None)),
        check_vma=False,
    )
```

```python
import functools

import jax
import jax.numpy as jnp
from jax import lax
from jax.experimental import pallas as pl
from jax.experimental.pallas import tpu as pltpu
from jax.sharding import PartitionSpec as P

eps_norm = 1e-06
VMEM = pl.BlockSpec(memory_space=pltpu.VMEM)
SMEM = pl.BlockSpec(memory_space=pltpu.SMEM)
HBM = pl.BlockSpec(memory_space=pltpu.HBM)
LIMIT = 24 * 2**20
PIECES = 4
LOG2_E = 1.4426950408889634
CUTS = 1


def along(value, axis, target):
    count = lax.axis_size(axis)
    pairs = [(source, target(source) % count) for source in range(count)]
    return lax.ppermute(value, axis, pairs)


def inverse_norm(values):
    return lax.rsqrt(jnp.sum(values * values, axis=-1, keepdims=True) + eps_norm)


def unit_half(raw):
    values = raw.astype(jnp.float32)
    return (values * inverse_norm(values)).astype(jnp.bfloat16)


def weigh(own, other, scale_ref):
    scores = lax.dot_general(
        own, other, (((1,), (1,)), ((), ())), preferred_element_type=jnp.float32
    )
    return jax.nn.sigmoid(scale_ref[0:1, 0:1] * scores + scale_ref[1:2, 0:1])


def visit(own, other, scale_ref):
    scores = lax.dot_general(
        own, other, (((1,), (1,)), ((), ())), preferred_element_type=jnp.float32
    )
    power = jnp.exp2(scale_ref[2:3, 0:1] * scores + scale_ref[3:4, 0:1])
    weights = scale_ref[0:1, 0:1] * pl.reciprocal(1.0 + power, approx=False)
    return jnp.dot(weights.astype(jnp.bfloat16), other, preferred_element_type=jnp.float32)


def odd_row():
    return lax.axis_index("row") & 1


def unit_back(raw, inverse, direction):
    values = raw.astype(jnp.float32)
    share = inverse * jnp.sum(values * direction, axis=-1, keepdims=True)
    return inverse * direction - values * (inverse * inverse * share)


def pieces(rows, count=PIECES):
    if rows % (16 * count):
        return [(0, rows)]
    return [(n * rows // count, rows // count) for n in range(count)]


def cuts(block):
    return [
        jax.ShapeDtypeStruct((size,) + block.shape[1:], block.dtype)
        for _, size in pieces(block.shape[0], CUTS)
    ]


def call(kernel, out_shape, in_specs, out_specs, work=1000, **more):
    return pl.pallas_call(
        kernel,
        out_shape=out_shape,
        in_specs=in_specs,
        out_specs=out_specs,
        compiler_params=pltpu.CompilerParams(vmem_limit_bytes=LIMIT),
        cost_estimate=pl.CostEstimate(flops=work, bytes_accessed=work, transcendentals=0),
        **more,
    )


def pick_kernel(img_ref, txt_ref, out_ref, sems):
    def copy(source):
        parts = [pl.ds(start, size) for start, size in pieces(out_ref.shape[0])]
        copies = [
            pltpu.make_async_copy(source.at[at], out_ref.at[at], sems.at[n])
            for n, at in enumerate(parts)
        ]
        for one in copies:
            one.start()
        for one in copies:
            one.wait()

    odd = odd_row()

    @pl.when(odd == 1)
    def _():
        copy(txt_ref)

    @pl.when(odd != 1)
    def _():
        copy(img_ref)


def pick(img, txt):
    return call(
        pick_kernel,
        jax.ShapeDtypeStruct(img.shape, img.dtype),
        [HBM, HBM],
        VMEM,
        scratch_shapes=[pltpu.SemaphoreType.DMA((len(pieces(img.shape[0])),))],
        name="pick",
    )(img, txt)


def load(sources, raw_refs, sems):
    parts = pieces(sources[0].shape[0])
    started = []
    for side, (source, raw_ref) in enumerate(zip(sources, raw_refs)):
        started.append([])
        for n, (start, size) in enumerate(parts):
            at = pl.ds(start, size)
            copy = pltpu.make_async_copy(source.at[at], raw_ref.at[at], sems.at[side, n])
            copy.start()
            started[-1].append((at, copy))
    return started


def norm_kernel(img_ref, img_half, raw_ref, sems):
    for at, copy in load((img_ref,), (raw_ref,), sems)[0]:
        copy.wait()
        img_half[at] = unit_half(raw_ref[at])


def norm(img):
    one = jax.ShapeDtypeStruct(img.shape, jnp.bfloat16)
    return call(
        norm_kernel,
        one,
        [HBM],
        VMEM,
        scratch_shapes=[
            pltpu.VMEM(img.shape, jnp.bfloat16),
            pltpu.SemaphoreType.DMA((1, len(pieces(img.shape[0])))),
        ],
        name="norm",
    )(img)


def own_kernel(
    exponent_ref, offset_ref, img_ref, txt_ref, img_half,
    scale_ref, raw_ref, half_ref, inverse_ref, near_ref, dir_ref, sems,
):
    started = load((img_ref, txt_ref), (raw_ref.at[0], raw_ref.at[1]), sems)
    scale_ref[0:1] = jnp.exp(jnp.broadcast_to(exponent_ref[...], (1, 128)))
    scale_ref[1:2] = jnp.broadcast_to(offset_ref[...], (1, 128))
    scale_ref[2:4] = -LOG2_E * scale_ref[0:2]
    half_ref[0] = img_half[...]
    for side in (1, 0):
        for at, copy in started[side]:
            copy.wait()
            values = raw_ref[side, at].astype(jnp.float32)
            inverse = inverse_norm(values)
            inverse_ref[side, at] = jnp.broadcast_to(inverse, (values.shape[0], 128))
            if side == 1:
                half_ref[1, at] = (values * inverse).astype(jnp.bfloat16)
    near_ref[...] = half_ref[1 - odd_row()]
    img, txt = half_ref[0], half_ref[1]
    rows = img.shape[0]
    row = lax.broadcasted_iota(jnp.int32, (rows, rows), 0)
    column = lax.broadcasted_iota(jnp.int32, (rows, rows), 1)
    match = jnp.where(row == column, 1.0, 0.0)
    for side, (own, other) in enumerate(((img, txt), (txt, img))):
        weights = scale_ref[0:1, 0:1] * (weigh(own, other, scale_ref) - match)
        dir_ref[side] = jnp.dot(
            weights.astype(jnp.bfloat16), other, preferred_element_type=jnp.float32
        )


def own_visit(exponent, offset, img, txt, img_half):
    rows, width = img.shape
    both = jax.ShapeDtypeStruct((2, rows, width), jnp.bfloat16)
    return call(
        own_kernel,
        (
            jax.ShapeDtypeStruct((8, 128), jnp.float32),
            both,
            both,
            jax.ShapeDtypeStruct((2, rows, 128), jnp.float32),
            jax.ShapeDtypeStruct((rows, width), jnp.bfloat16),
            jax.ShapeDtypeStruct((2, rows, width), jnp.float32),
        ),
        [VMEM, VMEM, HBM, HBM, VMEM],
        (VMEM,) * 6,
        scratch_shapes=[pltpu.SemaphoreType.DMA((2, len(pieces(rows))))],
        name="own",
    )(exponent.reshape(1, 1), offset.reshape(1, 1), img, txt, img_half)


def parts_of(kinds, refs, rows):
    refs, blocks = list(refs), []
    for _ in kinds:
        block = [refs.pop(0)]
        while sum(part.shape[0] for part in block) < rows:
            block.append(refs.pop(0))
        blocks.append(block)
    return blocks


def flat(entries):
    kinds = tuple(kind for kind, _ in entries)
    return kinds, jax.tree.leaves([block for _, block in entries])


def visit_all(kinds, blocks, scale_ref, half_ref, dir_ref, acc_ref, others_ref, sides=(0, 1)):
    rows = half_ref.shape[1]
    blocks = parts_of(kinds, blocks, rows)
    pairs = sum(side == 2 for side, _ in kinds)
    counts = [sum(kind[0] == side for kind in kinds) + pairs for side in (0, 1)]
    placed = [0, 0, 0, 0]
    for (side, raw), block in zip(kinds, blocks):
        if side < 2:
            slot = side * counts[0] + placed[side]
        else:
            to = odd_row() if side == 2 else 1 - odd_row()
            ends = [counts[0] - pairs + placed[side], sum(counts) - pairs + placed[side]]
            slot = ends[0] + to * (ends[1] - ends[0])
        placed[side] += 1
        start = slot * rows
        for part in block:
            size = part.shape[0]
            at = start if isinstance(start, int) else pl.multiple_of(start, 16)
            others_ref[pl.ds(at, size)] = unit_half(part[...]) if raw else part[...]
            start += size
    for side in sides:
        if counts[side]:
            others = others_ref[pl.ds(side * counts[0] * rows, counts[side] * rows)]
            acc_ref[side] = dir_ref[side] + visit(half_ref[side], others, scale_ref)
        else:
            acc_ref[side] = dir_ref[side]


def more_kernel(kinds, given, scale_ref, half_ref, dir_ref, *rest):
    blocks, rest = rest[: len(rest) - 2 - given], rest[len(rest) - 2 - given :]
    out_ref, halves, others_ref = rest[0], rest[1:-1], rest[-1]
    visit_all(kinds, blocks, scale_ref, half_ref, dir_ref, out_ref, others_ref)
    start = 0
    for cut in halves:
        cut[...] = others_ref[pl.ds(start, cut.shape[0])]
        start += cut.shape[0]


def finish(raw_ref, inverse_ref, acc_ref, grad_ref, held_ref, sems):
    copies = []
    for n, (start, size) in enumerate(pieces(held_ref.shape[0])):
        at = pl.ds(start, size)
        held_ref[at] = unit_back(raw_ref[at], inverse_ref[at][:, 0:1], acc_ref[at])
        copies.append(pltpu.make_async_copy(held_ref.at[at], grad_ref.at[at], sems.at[n]))
        copies[-1].start()
    return copies


def last_kernel(kinds, scale_ref, half_ref, dir_ref, raw_ref, inverse_ref, *rest):
    blocks, (img_grad, txt_grad, acc_ref, others_ref, held_ref, sems) = rest[:-6], rest[-6:]
    texts = any(side == 0 for side, _ in kinds)
    if texts:
        visit_all(kinds, blocks, scale_ref, half_ref, dir_ref, acc_ref, others_ref)
    source = acc_ref if texts else dir_ref
    copies = finish(
        raw_ref.at[0], inverse_ref.at[0], source.at[0], img_grad, held_ref.at[0], sems.at[0]
    )
    if not texts:
        visit_all(kinds, blocks, scale_ref, half_ref, dir_ref, acc_ref, others_ref, (1,))
    copies += finish(
        raw_ref.at[1], inverse_ref.at[1], acc_ref.at[1], txt_grad, held_ref.at[1], sems.at[1]
    )
    for copy in copies:
        copy.wait()


def more_visits(scale, half, direction, entries, give=False, work=1000):
    kinds, blocks = flat(entries)
    rows, width = half.shape[1:]
    one = jax.ShapeDtypeStruct((rows, width), jnp.bfloat16)
    halves = cuts(one) * len(kinds) if give else []
    direction, *halves = call(
        functools.partial(more_kernel, kinds, len(halves)),
        (jax.ShapeDtypeStruct(direction.shape, direction.dtype), *halves),
        [VMEM] * (3 + len(blocks)),
        (VMEM,) * (1 + len(halves)),
        scratch_shapes=[pltpu.VMEM((len(kinds) * rows, width), jnp.bfloat16)],
        input_output_aliases={2: 0},
        work=work,
        name="more",
    )(scale, half, direction, *blocks)
    return (direction, halves) if give else direction


def unit_kernel(raw_ref, half_ref):
    half_ref[...] = unit_half(raw_ref[...])


def normalized(raw):
    return call(unit_kernel, jax.ShapeDtypeStruct(raw.shape, raw.dtype), [VMEM], VMEM, name="unit")(raw)


def last_visits(scale, half, direction, raw, inverse, entries):
    kinds, blocks = flat(entries)
    rows, width = half.shape[1:]
    grad = jax.ShapeDtypeStruct((rows, width), jnp.float32)
    return call(
        functools.partial(last_kernel, kinds),
        (grad, grad),
        [VMEM] * (5 + len(blocks)),
        (HBM, HBM),
        scratch_shapes=[
            pltpu.VMEM(direction.shape, direction.dtype),
            pltpu.VMEM((max(1, len(kinds)) * rows, width), jnp.bfloat16),
            pltpu.VMEM(direction.shape, direction.dtype),
            pltpu.SemaphoreType.DMA((2, len(pieces(rows)))),
        ],
        name="last",
    )(scale, half, direction, raw, inverse, *blocks)


def tied(entries, *others):
    blocks, others = lax.optimization_barrier(([block for _, block in entries], others))
    return [(kind, block) for (kind, _), block in zip(entries, blocks)], *others


def on_device(
    picture_encoder_output, caption_encoder_output, softness_factor_exponent, logit_offset_term
):
    img, txt = picture_encoder_output, caption_encoder_output
    row_extent = min(8, lax.axis_size("row") // 2)
    column_extent = min(4, lax.axis_size("col") // 2)
    paired = row_extent % 2 == 0 and lax.axis_size("row") % 2 == 0
    swap = lambda s: s ^ 1
    held = [pltpu.with_memory_space_constraint(a, pltpu.HBM) for a in (img, txt)]
    text_cols, image_cols, text_rows, image_rows, swapped, last = [], [], [], [], [], []
    for k in range(1, column_extent):
        text_cols.append(((0, True), along(txt, "col", lambda s: s + k)))
    img_half = norm(held[0])
    for k in range(1, column_extent):
        image_cols.append(((1, False), along(img_half, "col", lambda s: s - k)))
    scale, raw, half, inverse, near, direction = own_visit(
        softness_factor_exponent, logit_offset_term, *held, img_half
    )
    if not paired:
        for k in range(1, row_extent):
            text_rows.append(((0, True), along(txt, "row", lambda s: s + k)))
            image_rows.append(((1, False), along(img_half, "row", lambda s: s - k)))
        last = text_cols + image_cols + text_rows + image_rows
        return last_visits(scale, half, direction, raw, inverse, last)

    reach = row_extent - 1
    far = along(pick(*held), "row", lambda s: s + reach if s % 2 else s - reach)
    for d in range(2, row_extent, 2):
        text_rows.append(((0, True), along(txt, "row", lambda s: s + d)))
        image_rows.append(((1, False), along(img_half, "row", lambda s: s - d)))
    if text_cols:
        direction = more_visits(scale, half, direction, text_cols)
    if text_rows:
        direction, halves = more_visits(scale, half, direction, text_rows, give=True)
        per = len(halves) // len(text_rows)
        for n in range(len(text_rows)):
            block = halves[n * per : (n + 1) * per]
            swapped.append(((0, False), [along(cut, "row", swap) for cut in block]))
    near, direction = lax.optimization_barrier((near, direction))
    swapped.append(((3, False), along(near, "row", swap)))
    far, direction = lax.optimization_barrier((far, direction))
    middle = image_rows + image_cols + [((2, False), normalized(far))]
    middle, direction = tied(middle, direction)
    last = [(kind, along(block, "row", swap)) for kind, block in middle[: len(image_rows)]]
    direction = more_visits(scale, half, direction, middle + swapped, work=4000000)
    return last_visits(scale, half, direction, raw, inverse, last)


def solution(mesh):
    return jax.shard_map(
        on_device,
        mesh=mesh,
        in_specs=(P(("row", "col"), None), P(("row", "col"), None), P(), P()),
        out_specs=(P(("row", "col"), None), P(("row", "col"), None)),
        check_vma=False,
    )
```
